32 devices in a mesh: gx: 8 (over z, y), gy: 4 (over x, core).
Axes of the slice: x: 2, y: 2, z: 4, core: 2. Of those that a mesh axis runs over, the one named last changes fastest.
Arguments:
- feats: bfloat16 [8, 4, 16, 512, 128], P('gx', 'gy'), may hold values from -6 to 6
- voxel_mask: int32 [8, 4, 16, 512], P('gx', 'gy'), may hold values 0 or 1
- brick_coord: int32 [8, 4, 16, 3], P('gx', 'gy'), may hold values from 0 to 3, as said below
- brick_count: int32 [8, 4, 2], P('gx', 'gy'), may hold values from 5 to 8, as said below
- route: int32 [8, 4, 16, 2], P('gx', 'gy'), may hold values from 0 to 7, as said below
- conv_weight: bfloat16 [3456, 128], replicated, may hold values from -0.109375 to 0.109375
- down_weight: bfloat16 [1024, 128], replicated, may hold values from -0.1875 to 0.1875
- coarse_grad: bfloat16 [8, 4, 16, 64, 128], P('gx', 'gy'), may hold values from -24 to 24
Outputs:
- coarse: bfloat16 [8, 4, 16, 64, 128], P('gx', 'gy')
- feat_grad: bfloat16 [8, 4, 16, 512, 128], P('gx', 'gy')
- conv_grad: float32 [3456, 128], replicated
- down_grad: float32 [1024, 128], replicated
The draws below stay inside these ranges and needn't reach their ends.
Inputs may be any that keep to these rules, and one draw needn't show every extreme that they name: `brick_coord`: each slot names a brick position inside its device's tile of 4 x 4 x 4 bricks. The first 8 slots of a device hold distinct positions in the tile's outer brick columns (x or y equal to 0 or 3); the other slots hold distinct positions in the inner columns. `brick_count`: occupied slots come first in each half; some device has all its slots occupied. `route`: all slots of one device have distinct pairs (owner, place), so a device sends at most 2 sub-bricks to one owner; in every gy row one owner receives 2 sub-bricks from every device of the row.
All inputs are finite; a program needn't handle non-finite values. No bound on the sum of `voxel_mask` on one device may be relied on, other than what follows from the above.
Results may differ from the reference program's by a relative error of at most 0.005.
Values may be sent and summed in bfloat16 or wider, within the bound.
A program may use at most 256 MiB of HBM per device.

```python
import math
import jax
import jax.numpy as jnp
import numpy as np
from jax import lax

CH = 128
EDGE = 8
VOX = 512
TILE = 4
DEPTH = 4
SLOTS = 16
BORDER = 8
CAP = 2
TILES_X = 8
TILES_Y = 4
RECV = 16


def outer_cells():
    found = [(x, y, z) for x in range(TILE) for y in range(TILE) for z in range(DEPTH) if x == 0 or y == 0 or x == TILE - 1 or (y == TILE - 1)]
    return np.array(found, dtype=np.int32)


def inner_cells():
    found = [(x, y, z) for x in range(1, TILE - 1) for y in range(1, TILE - 1) for z in range(DEPTH)]
    return np.array(found, dtype=np.int32)


def draw_brick_coord(key, part):
    key = jax.random.fold_in(key, 11)
    outer = jnp.asarray(outer_cells())
    inner = jnp.asarray(inner_cells())
    devices_total = TILES_X * TILES_Y
    keys_outer = jax.random.split(jax.random.fold_in(key, 1), devices_total)
    keys_inner = jax.random.split(jax.random.fold_in(key, 2), devices_total)
    pick_outer = jax.vmap(lambda k: jax.random.permutation(k, outer.shape[0])[:BORDER])(keys_outer)
    pick_inner = jax.vmap(lambda k: jax.random.permutation(k, inner.shape[0])[:BORDER])(keys_inner)
    coords = jnp.concatenate([outer[pick_outer], inner[pick_inner]], axis=1)
    return coords.reshape(TILES_X, TILES_Y, SLOTS, 3).astype(jnp.int32)


def draw_brick_count(key, part):
    key = jax.random.fold_in(key, 12)
    devices_total = TILES_X * TILES_Y
    lowest = max(1, BORDER - 3)
    counts = jax.random.randint(jax.random.fold_in(key, 1), (devices_total, 2), lowest, BORDER + 1)
    chosen = jax.random.randint(jax.random.fold_in(key, 2), (), 0, devices_total)
    filled = jnp.arange(devices_total, dtype=jnp.int32)[:, None] == chosen
    counts = jnp.where(filled, BORDER, counts)
    return counts.reshape(TILES_X, TILES_Y, 2).astype(jnp.int32)


def draw_route(key, part):
    key = jax.random.fold_in(key, 13)
    busy = jax.random.randint(jax.random.fold_in(key, 1), (TILES_Y,), 0, TILES_X).astype(jnp.int32)
    spare = (TILES_X - 1) * CAP
    keys_all = jax.random.split(jax.random.fold_in(key, 2), TILES_X * TILES_Y)
    picks = jax.vmap(lambda k: jax.random.permutation(k, spare)[:SLOTS - 2])(keys_all)
    picks = picks.reshape(TILES_X, TILES_Y, SLOTS - 2).astype(jnp.int32)
    hot = busy[None, :, None]
    other_owner = picks // CAP
    other_owner = other_owner + (other_owner >= hot).astype(jnp.int32)
    other_place = picks % CAP
    rest_slots = np.array([s for s in range(SLOTS) if s != 0 and s != BORDER], dtype=np.int32)
    owner = jnp.zeros((TILES_X, TILES_Y, SLOTS), jnp.int32)
    place = jnp.zeros((TILES_X, TILES_Y, SLOTS), jnp.int32)
    owner = owner.at[:, :, rest_slots].set(other_owner)
    place = place.at[:, :, rest_slots].set(other_place)
    busy_plane = jnp.broadcast_to(busy[None, :], (TILES_X, TILES_Y))
    owner = owner.at[:, :, 0].set(busy_plane).at[:, :, BORDER].set(busy_plane)
    place = place.at[:, :, 0].set(0).at[:, :, BORDER].set(1)
    return jnp.stack([owner, place], axis=-1).astype(jnp.int32)


def touch_ends(drawn, key, smallest, largest):
    shape = drawn.shape
    spot = [jax.random.randint(jax.random.fold_in(key, axis), (), 0, shape[axis]) for axis in range(len(shape))]
    drawn = drawn.at[tuple(spot)].set(smallest)
    longest = shape.index(max(shape))
    spot[longest] = (spot[longest] + 1) % shape[longest]
    return drawn.at[tuple(spot)].set(largest)


def steps_of(key, shape, cuts, least, high):
    gain = 1.0
    for axis_at, blocks in cuts:
        heights = jax.random.uniform(jax.random.fold_in(jax.random.fold_in(key, 6), axis_at), (blocks,), jnp.float32, least / len(cuts), high / len(cuts))
        gain = gain * jnp.repeat(jnp.exp(heights), shape[axis_at] // blocks).reshape((-1,) + (1,) * (len(shape) - 1 - axis_at))
    return gain


def noise(stream_key, dims, deviation, most, shards=(), held_as=jnp.bfloat16):
    drawn = deviation * jax.random.normal(stream_key, dims, jnp.float32)
    if shards:
        drawn = drawn * steps_of(stream_key, dims, shards, -0.22, 0.18)
    return jnp.clip(drawn, -most, most).astype(held_as)


def setup_inputs(seed: int = 0) -> dict:
    key_list = jax.random.split(jax.random.key(seed), 9)
    return {
        "feats": noise(key_list[0], (TILES_X, TILES_Y, SLOTS, VOX, CH), 1.0, 6.0, ((0, 8), (1, 4))),
        "voxel_mask": touch_ends((jax.random.randint(key_list[1], (TILES_X, TILES_Y, SLOTS, VOX), 0, 4) < 3).astype(jnp.int32), jax.random.fold_in(key_list[1], 1), 0, 1),
        "brick_coord": draw_brick_coord(jax.random.fold_in(key_list[8], 71), 0),
        "brick_count": draw_brick_count(jax.random.fold_in(key_list[8], 71), 0),
        "route": draw_route(jax.random.fold_in(key_list[8], 71), 0),
        "conv_weight": noise(key_list[5], (27 * CH, CH), (27 * CH) ** -0.5, 0.109375),
        "down_weight": noise(key_list[6], (8 * CH, CH), (8 * CH) ** -0.5, 0.1875),
        "coarse_grad": noise(key_list[7], (TILES_X, TILES_Y, RECV, VOX // 8, CH), 4.0, 24.0, ((0, 8), (1, 4))),
    }


def tap_offsets():
    return np.array([[a - 1, b - 1, c - 1] for a in range(3) for b in range(3) for c in range(3)], dtype=np.int32)

def unfold_taps(brick_pool, neighbour_index):
    edge = EDGE
    width = brick_pool.shape[-1]
    nearby = jnp.take(brick_pool, neighbour_index, axis=0)
    nearby = nearby.reshape(3, 3, 3, edge, edge, edge, width)
    nearby = nearby.transpose(0, 3, 1, 4, 2, 5, 6).reshape(3 * edge, 3 * edge, 3 * edge, width)
    padded = nearby[edge - 1:2 * edge + 1, edge - 1:2 * edge + 1, edge - 1:2 * edge + 1]
    columns = [padded[a:a + edge, b:b + edge, c:c + edge] for a in range(3) for b in range(3) for c in range(3)]
    return jnp.stack(columns, axis=3).reshape(edge ** 3, 27 * width)

def pool_pairs(activated):
    count = activated.shape[0]
    half = EDGE // 2
    blocks = activated.reshape(count, half, 2, half, 2, half, 2, CH).transpose(0, 1, 3, 5, 2, 4, 6, 7)
    return blocks.reshape(count * half ** 3, 8 * CH)

def unpool_pairs(columns, count):
    half = EDGE // 2
    blocks = columns.reshape(count, half, half, half, 2, 2, 2, CH).transpose(0, 1, 4, 2, 5, 3, 6, 7)
    return blocks.reshape(count, VOX, CH)

def reference(feats, voxel_mask, brick_coord, brick_count, route, conv_weight, down_weight, coarse_grad):
    tiles_x = TILES_X
    tiles_y = TILES_Y
    total_slots = tiles_x * tiles_y * SLOTS
    quarter = VOX // 8
    slot_ids = jnp.arange(SLOTS, dtype=jnp.int32)
    occupied = jnp.where(slot_ids < BORDER, slot_ids < brick_count[:, :, 0:1], slot_ids - BORDER < brick_count[:, :, 1:2])
    active = voxel_mask.astype(jnp.float32) * occupied.astype(jnp.float32)[..., None]
    inputs = feats * active.astype(jnp.bfloat16)[..., None]
    tile_i = jnp.arange(tiles_x, dtype=jnp.int32)[:, None, None]
    tile_j = jnp.arange(tiles_y, dtype=jnp.int32)[None, :, None]
    glob_x = brick_coord[..., 0] + TILE * tile_i
    glob_y = brick_coord[..., 1] + TILE * tile_j
    glob_z = brick_coord[..., 2]
    span_y = TILE * tiles_y + 2
    span_z = DEPTH + 2
    cells = (TILE * tiles_x + 2) * span_y * span_z
    position = ((glob_x + 1) * span_y + glob_y + 1) * span_z + glob_z + 1
    position = jnp.where(occupied, position, cells).reshape(-1).astype(jnp.int32)
    lookup = jnp.full((cells + 1,), total_slots, jnp.int32).at[position].set(jnp.arange(total_slots, dtype=jnp.int32))
    offsets = jnp.asarray(tap_offsets())
    flat_x = glob_x.reshape(-1, 1)
    flat_y = glob_y.reshape(-1, 1)
    flat_z = glob_z.reshape(-1, 1)
    wanted = ((flat_x + 1 + offsets[:, 0]) * span_y + flat_y + 1 + offsets[:, 1]) * span_z + flat_z + 1 + offsets[:, 2]
    neighbour_index = lookup[wanted.astype(jnp.int32)]
    empty_brick = jnp.zeros((1, VOX, CH), jnp.bfloat16)
    brick_pool = jnp.concatenate([inputs.reshape(total_slots, VOX, CH), empty_brick], axis=0)
    flat_active = active.reshape(total_slots, VOX)

    def forward_one(row_index):
        return jnp.dot(unfold_taps(brick_pool, row_index), conv_weight, preferred_element_type=jnp.float32)
    preact = lax.map(forward_one, neighbour_index)
    activated = (jax.nn.silu(preact) * flat_active[..., None]).astype(jnp.bfloat16)
    block_rows = pool_pairs(activated)
    sub_rows = jnp.dot(block_rows, down_weight, preferred_element_type=jnp.float32).astype(jnp.bfloat16)
    received_count = CAP * tiles_x
    owner = route[..., 0]
    place = route[..., 1]
    target = (owner * tiles_y + tile_j) * received_count + tile_i * CAP + place
    dump = tiles_x * tiles_y * received_count
    target = jnp.where(occupied, target, dump).reshape(-1).astype(jnp.int32)
    coarse = jnp.zeros((dump + 1, quarter, CH), jnp.bfloat16).at[target].set(sub_rows.reshape(total_slots, quarter, CH))
    coarse = coarse[:dump].reshape(tiles_x, tiles_y, received_count, quarter, CH)
    grad_flat = jnp.concatenate([coarse_grad.reshape(dump, quarter, CH), jnp.zeros((1, quarter, CH), jnp.bfloat16)], axis=0)
    grad_rows = grad_flat[target].reshape(total_slots * quarter, CH)
    down_grad = lax.dot_general(block_rows, grad_rows, (((0,), (0,)), ((), ())), preferred_element_type=jnp.float32)
    back_rows = jnp.dot(grad_rows, down_weight.T, preferred_element_type=jnp.float32)
    grad_act = unpool_pairs(back_rows, total_slots)
    sigmoid_z = jax.nn.sigmoid(preact)
    grad_pre = (grad_act * flat_active[..., None] * sigmoid_z * (1.0 + preact * (1.0 - sigmoid_z))).astype(jnp.bfloat16)
    grad_pool = jnp.concatenate([grad_pre, empty_brick], axis=0)
    flipped = conv_weight.reshape(27, CH, CH)[::-1].transpose(0, 2, 1).reshape(27 * CH, CH)

    def backward_one(running, item):
        row_index, grad_slot = item
        running = running + lax.dot_general(unfold_taps(brick_pool, row_index), grad_slot, (((0,), (0,)), ((), ())), preferred_element_type=jnp.float32)
        back = jnp.dot(unfold_taps(grad_pool, row_index), flipped, preferred_element_type=jnp.float32)
        return (running, back)
    conv_grad, back_all = lax.scan(backward_one, jnp.zeros((27 * CH, CH), jnp.float32), (neighbour_index, grad_pre))
    feat_grad = (back_all * flat_active[..., None]).astype(jnp.bfloat16).reshape(feats.shape)
    conv_grad = conv_grad * (1.0 / math.sqrt(total_slots * VOX))
    down_grad = down_grad * (1.0 / math.sqrt(total_slots * VOX // 8))
    return (coarse, feat_grad, conv_grad, down_grad)
```

```python
import math

import jax
import jax.numpy as jnp
import numpy as np
from jax import lax
from jax.experimental import pallas as pl
from jax.experimental.pallas import tpu as pltpu
from jax.sharding import PartitionSpec as P

CH = 128
EDGE = 8
VOX = 512
TILE = 4
SLOTS = 16
BORDER = 8
CAP = 2
SPAN = TILE * EDGE
FACE = SPAN * SPAN
BF = jnp.bfloat16
F32 = jnp.float32
VM = pl.BlockSpec(memory_space=pltpu.VMEM)
SM = pl.BlockSpec(memory_space=pltpu.SMEM)
LIMIT = 60 * 1024 * 1024


def pool_order():
    order = (
        np.arange(VOX).reshape(4, 2, 4, 2, 4, 2).transpose(1, 3, 5, 0, 2, 4).reshape(-1)
    )
    matrix = np.zeros((VOX, VOX), np.float32)
    matrix[np.arange(VOX), order] = 1.0
    return matrix


def put_faces(faces, cube, x, y, z):
    @pl.when(x == 0)
    def _():
        faces[0, pl.ds(y * EDGE, EDGE), z] = cube[0]

    @pl.when(x == TILE - 1)
    def _():
        faces[1, pl.ds(y * EDGE, EDGE), z] = cube[EDGE - 1]

    @pl.when(y == 0)
    def _():
        faces[2, pl.ds(x * EDGE, EDGE), z] = cube[:, 0]

    @pl.when(y == TILE - 1)
    def _():
        faces[3, pl.ds(x * EDGE, EDGE), z] = cube[:, EDGE - 1]


def face_kernel(coord, feats, mask, out, faces):
    faces[...] = jnp.zeros_like(faces)

    def body(s, carry):
        cube = (feats[s].astype(F32) * mask[s].astype(F32)).reshape(EDGE, EDGE, EDGE, CH)
        put_faces(faces, cube, coord[s, 0], coord[s, 1], coord[s, 2])
        return carry

    lax.fori_loop(0, BORDER, body, 0)
    out[...] = faces[...].reshape(4, FACE, CH).astype(BF)


def fill_volume(volume, halo, corners):
    def clear(i, carry):
        volume[i] = jnp.zeros(volume.shape[1:], F32)
        return carry

    lax.fori_loop(0, volume.shape[0], clear, 0)
    inner = slice(1, 1 + SPAN)
    depth = slice(1, 1 + TILE)
    plane = (SPAN, TILE, EDGE, CH)
    volume[0, inner, depth] = halo[0][...].astype(F32).reshape(plane)
    volume[1 + SPAN, inner, depth] = halo[1][...].astype(F32).reshape(plane)
    volume[inner, 0, depth] = halo[2][...].astype(F32).reshape(plane)
    volume[inner, 1 + SPAN, depth] = halo[3][...].astype(F32).reshape(plane)
    for at, (cx, cy) in enumerate(((0, 0), (0, 1), (1, 0), (1, 1))):
        line = corners[at][...].astype(F32).reshape(TILE, EDGE, CH)
        volume[cx * (1 + SPAN), cy * (1 + SPAN), depth] = line


def place_brick(volume, cube, x, y, z):
    volume[pl.ds(1 + x * EDGE, EDGE), pl.ds(1 + y * EDGE, EDGE), 1 + z] = cube


def unfold(volume, shifted, columns, x, y, z):
    ys = pl.ds(y * EDGE, EDGE + 2)
    row = lax.broadcasted_iota(jnp.int32, (EDGE, CH), 0)[None]

    def lines(i, carry):
        at = x * EDGE + i
        mid = volume[at, ys, z + 1]
        low = jnp.where(row == EDGE - 1, volume[at, ys, z], mid)
        high = jnp.where(row == 0, volume[at, ys, z + 2], mid)
        shifted[0, i] = pltpu.roll(low, 1, 1)
        shifted[1, i] = mid
        shifted[2, i] = pltpu.roll(high, EDGE - 1, 1)
        return carry

    lax.fori_loop(0, EDGE + 2, lines, 0, unroll=True)
    for tap in range(27):
        a, b, c = tap // 9, tap // 3 % 3, tap % 3
        piece = shifted[c, a : a + EDGE, b : b + EDGE].reshape(VOX, CH).astype(BF)
        columns[:, tap * CH : (tap + 1) * CH] = piece


def main_kernel(
    coord, target, feats, mask, halo, corners, returned, weight, down, gather, scatter,
    sending, grad_out, face_out, conv_out, down_out,
    volume, shifted, columns, faces, conv_acc, grads, back_rows, blocks,
):
    fill_volume(volume, halo, corners)
    faces[...] = jnp.zeros_like(faces)
    conv_acc[...] = jnp.zeros_like(conv_acc)
    sending[...] = jnp.zeros_like(sending)

    def place(s, carry):
        cube = (feats[s].astype(F32) * mask[s].astype(F32)).reshape(EDGE, EDGE, EDGE, CH)
        place_brick(volume, cube, coord[s, 0], coord[s, 1], coord[s, 2])
        rows = pl.ds(pl.multiple_of(s * 64, 64), 64)
        grads[rows] = returned[target[s]]
        return carry

    lax.fori_loop(0, SLOTS, place, 0)

    def spread(i, carry):
        rows = pl.ds(pl.multiple_of(i * 256, 256), 256)
        back_rows[rows] = lax.dot_general(
            grads[rows], down[...], (((1,), (1,)), ((), ())), preferred_element_type=F32
        )
        return carry

    lax.fori_loop(0, SLOTS // 4, spread, 0)

    def body(s, carry):
        x, y, z = coord[s, 0], coord[s, 1], coord[s, 2]
        rows = pl.ds(pl.multiple_of(s * 64, 64), 64)
        unfold(volume, shifted, columns, x, y, z)
        preact = jnp.dot(columns[...], weight[...], preferred_element_type=F32)
        active = mask[s].astype(F32)
        sig = jax.nn.sigmoid(preact)
        activated = (preact * sig * active).astype(BF)
        ordered = jnp.dot(gather[...], activated, preferred_element_type=F32).astype(BF)
        blocks[rows] = jnp.concatenate([ordered[64 * q : 64 * q + 64] for q in range(8)], axis=1)
        wide = back_rows[rows]
        tall = jnp.concatenate([wide[:, CH * q : CH * q + CH] for q in range(8)], axis=0)
        head = tall.astype(BF)
        rest = (tall - head.astype(F32)).astype(BF)
        both = jnp.dot(
            scatter[...], jnp.concatenate([head, rest], axis=1), preferred_element_type=F32
        )
        grad_act = both[:, :CH] + both[:, CH:]
        grad_f32 = grad_act * active * sig * (1.0 + preact * (1.0 - sig))
        grad = grad_f32.astype(BF)
        grad_out[s] = grad
        rounded = grad.astype(F32)

        @pl.when(s < BORDER)
        def _():
            put_faces(faces, rounded.reshape(EDGE, EDGE, EDGE, CH), x, y, z)

        turned = rounded.T.astype(BF)
        conv_acc[...] += jnp.dot(turned, columns[...], preferred_element_type=F32)
        return carry

    lax.fori_loop(0, SLOTS, body, 0)
    face_out[...] = faces[...].reshape(4, FACE, CH).astype(BF)
    for tap in range(27):
        conv_out[tap * CH : (tap + 1) * CH] = conv_acc[:, tap * CH : (tap + 1) * CH].T
    turned = grads[...].astype(F32).T.astype(BF)
    down_acc = jnp.dot(turned, blocks[...], preferred_element_type=F32)
    for q in range(8):
        down_out[q * CH : (q + 1) * CH] = down_acc[:, q * CH : (q + 1) * CH].T

    def send(s, carry):
        rows = pl.ds(pl.multiple_of(s * 64, 64), 64)
        sub = jnp.dot(blocks[rows], down[...], preferred_element_type=F32)
        sending[target[s]] = sub.astype(BF)
        return carry

    lax.fori_loop(0, SLOTS, send, 0)


def back_kernel(coord, grad, mask, halo, corners, weight, out, volume, shifted, columns):
    fill_volume(volume, halo, corners)

    def place(s, carry):
        cube = grad[s].astype(F32).reshape(EDGE, EDGE, EDGE, CH)
        place_brick(volume, cube, coord[s, 0], coord[s, 1], coord[s, 2])
        return carry

    lax.fori_loop(0, SLOTS, place, 0)

    def body(s, carry):
        unfold(volume, shifted, columns, coord[s, 0], coord[s, 1], coord[s, 2])
        back = jnp.dot(columns[...], weight[...], preferred_element_type=F32)
        out[s] = (back * mask[s].astype(F32)).astype(BF)
        return carry

    lax.fori_loop(0, SLOTS, body, 0)


VOLUME = pltpu.VMEM((SPAN + 2, SPAN + 2, TILE + 2, EDGE, CH), F32)
SHIFTED = pltpu.VMEM((3, EDGE + 2, EDGE + 2, EDGE, CH), F32)
COLUMNS = pltpu.VMEM((VOX, 27 * CH), BF)
FACES = pltpu.VMEM((4, SPAN, TILE, EDGE, CH), F32)


def swap_faces(faces):
    nx, ny = lax.axis_size("gx"), lax.axis_size("gy")
    up_x = [(i, i + 1) for i in range(nx - 1)]
    down_x = [(i + 1, i) for i in range(nx - 1)]
    up_y = [(j, j + 1) for j in range(ny - 1)]
    down_y = [(j + 1, j) for j in range(ny - 1)]
    halo = (
        lax.ppermute(faces[1], "gx", up_x),
        lax.ppermute(faces[0], "gx", down_x),
        lax.ppermute(faces[3], "gy", up_y),
        lax.ppermute(faces[2], "gy", down_y),
    )
    corners = []
    for cx in (0, 1):
        for cy in (0, 1):
            line = faces[1 - cx, FACE - SPAN :] if cy == 0 else faces[1 - cx, :SPAN]
            pairs = [
                (i * ny + j, (i + 1 - 2 * cx) * ny + j + 1 - 2 * cy)
                for i in range(nx)
                for j in range(ny)
                if 0 <= i + 1 - 2 * cx < nx and 0 <= j + 1 - 2 * cy < ny
            ]
            corners.append(lax.ppermute(line, ("gx", "gy"), pairs))
    return halo, corners


def unpack(kernel, at):
    def wrapped(*refs):
        kernel(*refs[:at], refs[at : at + 4], refs[at + 4 : at + 8], *refs[at + 8 :])

    return wrapped


def per_device(
    feats, voxel_mask, brick_coord, brick_count, route, conv_weight, down_weight, coarse_grad
):
    tiles_x = lax.axis_size("gx")
    tiles_y = lax.axis_size("gy")
    quarter = VOX // 8
    received = CAP * tiles_x
    params = pltpu.CompilerParams(vmem_limit_bytes=LIMIT)
    slot_ids = jnp.arange(SLOTS, dtype=jnp.int32)
    counts = brick_count[0, 0]
    occupied = jnp.where(slot_ids < BORDER, slot_ids < counts[0], slot_ids - BORDER < counts[1])
    mask = jnp.broadcast_to(
        jnp.where(occupied[:, None], voxel_mask[0, 0], 0).astype(BF)[:, :, None], (SLOTS, VOX, CH)
    )
    coord = brick_coord[0, 0]
    target = route[0, 0, :, 0] * CAP + route[0, 0, :, 1]
    feats = feats[0, 0]

    faces = pl.pallas_call(
        face_kernel,
        out_shape=jax.ShapeDtypeStruct((4, FACE, CH), BF),
        in_specs=[SM, VM, VM],
        out_specs=VM,
        scratch_shapes=[FACES],
        compiler_params=params,
    )(coord, feats, mask)
    returned = lax.all_to_all(
        coarse_grad[0, 0].reshape(tiles_x, CAP * quarter, CH),
        "gx", split_axis=0, concat_axis=0, tiled=True,
    ).reshape(received, quarter, CH)
    halo, corners = swap_faces(faces)
    order = pool_order()
    sending, grad_pre, grad_faces, conv_local, down_local = pl.pallas_call(
        unpack(main_kernel, 4),
        out_shape=(
            jax.ShapeDtypeStruct((received, quarter, CH), BF),
            jax.ShapeDtypeStruct((SLOTS, VOX, CH), BF),
            jax.ShapeDtypeStruct((4, FACE, CH), BF),
            jax.ShapeDtypeStruct((27 * CH, CH), F32),
            jax.ShapeDtypeStruct((8 * CH, CH), F32),
        ),
        in_specs=[SM, SM] + [VM] * 15,
        out_specs=(VM,) * 5,
        scratch_shapes=[
            VOLUME, SHIFTED, COLUMNS, FACES,
            pltpu.VMEM((CH, 27 * CH), F32),
            pltpu.VMEM((SLOTS * quarter, CH), BF),
            pltpu.VMEM((SLOTS * quarter, 8 * CH), F32),
            pltpu.VMEM((SLOTS * quarter, 8 * CH), BF),
        ],
        compiler_params=params,
        cost_estimate=pl.CostEstimate(
            flops=4 * SLOTS * VOX * 27 * CH * CH, bytes_accessed=16 << 20, transcendentals=0
        ),
    )(
        coord, target, feats, mask, *halo, *corners, returned, conv_weight, down_weight,
        jnp.asarray(order, BF), jnp.asarray(order.T, BF),
    )
    conv_sum, down_sum = lax.psum((conv_local, down_local), ("gx", "gy"))
    grad_halo, grad_corners = swap_faces(grad_faces)
    coarse = lax.all_to_all(
        sending.reshape(tiles_x, CAP * quarter, CH), "gx", split_axis=0, concat_axis=0, tiled=True
    ).reshape(1, 1, received, quarter, CH)
    flipped = conv_weight.reshape(27, CH, CH)[::-1].transpose(0, 2, 1).reshape(27 * CH, CH)
    feat_grad = pl.pallas_call(
        unpack(back_kernel, 3),
        out_shape=jax.ShapeDtypeStruct((SLOTS, VOX, CH), BF),
        in_specs=[SM] + [VM] * 11,
        out_specs=VM,
        scratch_shapes=[VOLUME, SHIFTED, COLUMNS],
        compiler_params=params,
        cost_estimate=pl.CostEstimate(
            flops=2 * SLOTS * VOX * 27 * CH * CH, bytes_accessed=8 << 20, transcendentals=0
        ),
    )(coord, grad_pre, mask, *grad_halo, *grad_corners, flipped)
    total_slots = tiles_x * tiles_y * SLOTS
    conv_grad = conv_sum * (1.0 / math.sqrt(total_slots * VOX))
    down_grad = down_sum * (1.0 / math.sqrt(total_slots * VOX // 8))
    return (coarse, feat_grad[None, None], conv_grad, down_grad)


def solution(mesh):
    in_specs = (
        P("gx", "gy", None, None, None),
        P("gx", "gy", None, None),
        P("gx", "gy", None, None),
        P("gx", "gy", None),
        P("gx", "gy", None, None),
        P(),
        P(),
        P("gx", "gy", None, None, None),
    )
    out_specs = (P("gx", "gy", None, None, None), P("gx", "gy", None, None, None), P(), P())
    return jax.shard_map(
        per_device, mesh=mesh, in_specs=in_specs, out_specs=out_specs, check_vma=False
    )
```

```python
import functools
import math

import jax
import jax.numpy as jnp
import numpy as np
from jax import lax
from jax.experimental import pallas as pl
from jax.experimental.pallas import tpu as pltpu
from jax.sharding import PartitionSpec as P

CH = 128
EDGE = 8
VOX = 512
TILE = 4
SLOTS = 16
BORDER = 8
CAP = 2
SPAN = TILE * EDGE
FACE = SPAN * SPAN
BF = jnp.bfloat16
F32 = jnp.float32
VM = pl.BlockSpec(memory_space=pltpu.VMEM)
SM = pl.BlockSpec(memory_space=pltpu.SMEM)
MESH = pl.DeviceIdType.MESH
LIMIT = 60 * 1024 * 1024


def pool_order():
    order = (
        np.arange(VOX).reshape(4, 2, 4, 2, 4, 2).transpose(1, 3, 5, 0, 2, 4).reshape(-1)
    )
    matrix = np.zeros((VOX, VOX), np.float32)
    matrix[np.arange(VOX), order] = 1.0
    return matrix


def put_faces(faces, cube, x, y, z):
    @pl.when(x == 0)
    def _():
        faces[0, pl.ds(y * EDGE, EDGE), z] = cube[0]

    @pl.when(x == TILE - 1)
    def _():
        faces[1, pl.ds(y * EDGE, EDGE), z] = cube[EDGE - 1]

    @pl.when(y == 0)
    def _():
        faces[2, pl.ds(x * EDGE, EDGE), z] = cube[:, 0]

    @pl.when(y == TILE - 1)
    def _():
        faces[3, pl.ds(x * EDGE, EDGE), z] = cube[:, EDGE - 1]


def face_kernel(coord, feats, mask, out, faces):
    faces[...] = jnp.zeros_like(faces)

    def body(s, carry):
        cube = (feats[s].astype(F32) * mask[s].astype(F32)).reshape(EDGE, EDGE, EDGE, CH)
        put_faces(faces, cube, coord[s, 0], coord[s, 1], coord[s, 2])
        return carry

    lax.fori_loop(0, BORDER, body, 0)
    out[...] = faces[...].reshape(4, FACE, CH).astype(BF)


def fill_volume(volume, halo, corners):
    def clear(i, carry):
        volume[i] = jnp.zeros(volume.shape[1:], F32)
        return carry

    lax.fori_loop(0, volume.shape[0], clear, 0)
    inner = slice(1, 1 + SPAN)
    depth = slice(1, 1 + TILE)
    plane = (SPAN, TILE, EDGE, CH)
    volume[0, inner, depth] = halo[0].astype(F32).reshape(plane)
    volume[1 + SPAN, inner, depth] = halo[1].astype(F32).reshape(plane)
    volume[inner, 0, depth] = halo[2].astype(F32).reshape(plane)
    volume[inner, 1 + SPAN, depth] = halo[3].astype(F32).reshape(plane)
    for at, (cx, cy) in enumerate(((0, 0), (0, 1), (1, 0), (1, 1))):
        line = corners[at].astype(F32).reshape(TILE, EDGE, CH)
        volume[cx * (1 + SPAN), cy * (1 + SPAN), depth] = line


def place_brick(volume, cube, x, y, z):
    volume[pl.ds(1 + x * EDGE, EDGE), pl.ds(1 + y * EDGE, EDGE), 1 + z] = cube


def unfold(volume, shifted, columns, x, y, z):
    ys = pl.ds(y * EDGE, EDGE + 2)
    row = lax.broadcasted_iota(jnp.int32, (EDGE, CH), 0)[None]

    def lines(i, carry):
        at = x * EDGE + i
        mid = volume[at, ys, z + 1]
        low = jnp.where(row == EDGE - 1, volume[at, ys, z], mid)
        high = jnp.where(row == 0, volume[at, ys, z + 2], mid)
        shifted[0, i] = pltpu.roll(low, 1, 1)
        shifted[1, i] = mid
        shifted[2, i] = pltpu.roll(high, EDGE - 1, 1)
        return carry

    lax.fori_loop(0, EDGE + 2, lines, 0, unroll=True)
    for tap in range(27):
        a, b, c = tap // 9, tap // 3 % 3, tap % 3
        piece = shifted[c, a : a + EDGE, b : b + EDGE].reshape(VOX, CH).astype(BF)
        columns[:, tap * CH : (tap + 1) * CH] = piece


def main_kernel(
    coord, target, feats, mask, halo, corners, returned, weight, down, gather, scatter,
    sending, grad_out, face_out, sums,
    volume, shifted, columns, faces, conv_acc, grads, back_rows, blocks,
):
    fill_volume(volume, halo, corners)
    faces[...] = jnp.zeros_like(faces)
    conv_acc[...] = jnp.zeros_like(conv_acc)
    sending[...] = jnp.zeros_like(sending)

    def place(s, carry):
        cube = (feats[s].astype(F32) * mask[s].astype(F32)).reshape(EDGE, EDGE, EDGE, CH)
        place_brick(volume, cube, coord[s, 0], coord[s, 1], coord[s, 2])
        rows = pl.ds(pl.multiple_of(s * 64, 64), 64)
        grads[rows] = returned[target[s]]
        return carry

    lax.fori_loop(0, SLOTS, place, 0)

    def spread(i, carry):
        rows = pl.ds(pl.multiple_of(i * 256, 256), 256)
        back_rows[rows] = lax.dot_general(
            grads[rows], down[...], (((1,), (1,)), ((), ())), preferred_element_type=F32
        )
        return carry

    lax.fori_loop(0, SLOTS // 4, spread, 0)

    def body(s, carry):
        x, y, z = coord[s, 0], coord[s, 1], coord[s, 2]
        rows = pl.ds(pl.multiple_of(s * 64, 64), 64)
        unfold(volume, shifted, columns, x, y, z)
        preact = jnp.dot(columns[...], weight[...], preferred_element_type=F32)
        active = mask[s].astype(F32)
        sig = jax.nn.sigmoid(preact)
        activated = (preact * sig * active).astype(BF)
        ordered = jnp.dot(gather[...], activated, preferred_element_type=F32).astype(BF)
        blocks[rows] = jnp.concatenate([ordered[64 * q : 64 * q + 64] for q in range(8)], axis=1)
        wide = back_rows[rows]
        tall = jnp.concatenate([wide[:, CH * q : CH * q + CH] for q in range(8)], axis=0)
        head = tall.astype(BF)
        rest = (tall - head.astype(F32)).astype(BF)
        both = jnp.dot(
            scatter[...], jnp.concatenate([head, rest], axis=1), preferred_element_type=F32
        )
        grad_act = both[:, :CH] + both[:, CH:]
        grad_f32 = grad_act * active * sig * (1.0 + preact * (1.0 - sig))
        grad = grad_f32.astype(BF)
        grad_out[s] = grad
        rounded = grad.astype(F32)

        @pl.when(s < BORDER)
        def _():
            put_faces(faces, rounded.reshape(EDGE, EDGE, EDGE, CH), x, y, z)

        turned = rounded.T.astype(BF)
        conv_acc[...] += jnp.dot(turned, columns[...], preferred_element_type=F32)
        return carry

    lax.fori_loop(0, SLOTS, body, 0)
    face_out[...] = faces[...].reshape(4, FACE, CH).astype(BF)
    for tap in range(27):
        sums[tap * CH : (tap + 1) * CH] = conv_acc[:, tap * CH : (tap + 1) * CH].T.astype(BF)
    turned = grads[...].astype(F32).T.astype(BF)
    down_acc = jnp.dot(turned, blocks[...], preferred_element_type=F32)
    for q in range(8):
        rows = slice((27 + q) * CH, (28 + q) * CH)
        sums[rows] = down_acc[:, q * CH : (q + 1) * CH].T.astype(BF)
    if sums.shape[0] > 35 * CH:
        sums[35 * CH :] = jnp.zeros((sums.shape[0] - 35 * CH, CH), BF)

    def send(s, carry):
        rows = pl.ds(pl.multiple_of(s * 64, 64), 64)
        sub = jnp.dot(blocks[rows], down[...], preferred_element_type=F32)
        sending[target[s]] = sub.astype(BF)
        return carry

    lax.fori_loop(0, SLOTS, send, 0)


def back_kernel(coord, grad, mask, halo, corners, weight, out, volume, shifted, columns):
    fill_volume(volume, halo, corners)

    def place(s, carry):
        cube = grad[s].astype(F32).reshape(EDGE, EDGE, EDGE, CH)
        place_brick(volume, cube, coord[s, 0], coord[s, 1], coord[s, 2])
        return carry

    lax.fori_loop(0, SLOTS, place, 0)

    def body(s, carry):
        unfold(volume, shifted, columns, coord[s, 0], coord[s, 1], coord[s, 2])
        back = jnp.dot(columns[...], weight[...], preferred_element_type=F32)
        out[s] = (back * mask[s].astype(F32)).astype(BF)
        return carry

    lax.fori_loop(0, SLOTS, body, 0)


VOLUME = pltpu.VMEM((SPAN + 2, SPAN + 2, TILE + 2, EDGE, CH), F32)
SHIFTED = pltpu.VMEM((3, EDGE + 2, EDGE + 2, EDGE, CH), F32)
COLUMNS = pltpu.VMEM((VOX, 27 * CH), BF)
FACES = pltpu.VMEM((4, SPAN, TILE, EDGE, CH), F32)


def at_rows(start, size):
    return pl.ds(pl.multiple_of(start, 16), size)


def greet(peers):
    barrier = pltpu.get_barrier_semaphore()
    for peer in peers:
        pl.semaphore_signal(barrier, inc=1, device_id=peer, device_id_type=MESH)
    pl.semaphore_wait(barrier, len(peers))


def around(nx, ny, gx, gy):
    ring = [
        (lax.rem(gx + dx + nx, nx), lax.rem(gy + dy + ny, ny))
        for dx in (-1, 0, 1)
        for dy in (-1, 0, 1)
        if dx or dy
    ]
    return ring + [(lax.rem(gx + k, nx), gy) for k in range(1, nx)]


def border_copies(nx, ny, gx, gy, faces, halo, corners, send, recv):
    plan = [
        (1, 0, faces.at[1], halo.at[0]),
        (-1, 0, faces.at[0], halo.at[1]),
        (0, 1, faces.at[3], halo.at[2]),
        (0, -1, faces.at[2], halo.at[3]),
    ]
    for at, (cx, cy) in enumerate(((0, 0), (0, 1), (1, 0), (1, 1))):
        rows = pl.ds(FACE - SPAN if cy == 0 else 0, SPAN)
        plan.append((1 - 2 * cx, 1 - 2 * cy, faces.at[1 - cx, rows], corners.at[at]))
    copies = []
    for at, (dx, dy, source, place) in enumerate(plan):
        sends = (gx + dx >= 0) & (gx + dx < nx) & (gy + dy >= 0) & (gy + dy < ny)
        gets = (gx - dx >= 0) & (gx - dx < nx) & (gy - dy >= 0) & (gy - dy < ny)
        copy = pltpu.make_async_remote_copy(
            src_ref=source, dst_ref=place, send_sem=send.at[at], recv_sem=recv.at[at],
            device_id=(lax.rem(gx + dx + nx, nx), lax.rem(gy + dy + ny, ny)),
            device_id_type=MESH,
        )
        copies.append((copy, place, sends, gets))
    return copies


def start_border(copies):
    for copy, place, sends, gets in copies:

        @pl.when(sends)
        def _(copy=copy):
            copy.start()

        @pl.when(jnp.logical_not(gets))
        def _(place=place):
            place[...] = jnp.zeros(place.shape, BF)


def wait_border(copies):
    for copy, place, sends, gets in copies:

        @pl.when(sends)
        def _(copy=copy):
            copy.wait_send()

        @pl.when(gets)
        def _(copy=copy):
            copy.wait_recv()


def trade_copies(nx, gx, gy, source, place, send, recv):
    block = source.shape[0] // nx
    copies = []
    for k in range(1, nx):
        peer = lax.rem(gx + k, nx)
        copies.append(
            pltpu.make_async_remote_copy(
                src_ref=source.at[at_rows(peer * block, block)],
                dst_ref=place.at[at_rows(gx * block, block)],
                send_sem=send.at[k - 1], recv_sem=recv.at[k - 1],
                device_id=(peer, gy), device_id_type=MESH,
            )
        )
    return copies


def keep_own(nx, gx, source, place):
    block = source.shape[0] // nx
    place[at_rows(gx * block, block)] = source[at_rows(gx * block, block)]


def early_kernel(nx, ny, faces, cotangent, halo, corners, returned, send, recv, tsend, trecv):
    gx, gy = lax.axis_index("gx"), lax.axis_index("gy")
    greet(around(nx, ny, gx, gy))
    border = border_copies(nx, ny, gx, gy, faces, halo, corners, send, recv)
    trade = trade_copies(nx, gx, gy, cotangent, returned, tsend, trecv)
    start_border(border)
    for copy in trade:
        copy.start()
    keep_own(nx, gx, cotangent, returned)
    wait_border(border)
    for copy in trade:
        copy.wait()


def late_kernel(
    nx, ny, faces, sending, sums, halo, corners, coarse, total,
    pair_in, line_in, row_in, pair_sum, line_sum, send, recv, tsend, trecv, ssend, srecv,
):
    gx, gy = lax.axis_index("gx"), lax.axis_index("gy")
    core, line, lines = lax.rem(gy, 2), gy // 2, ny // 2
    half = sums.shape[0] // 2
    part = half // lines
    unit = part // nx
    mate = (gx, gy + 1 - 2 * core)
    beside = [lax.rem(line + k, lines) for k in range(1, lines)]
    along = [lax.rem(gx + k, nx) for k in range(1, nx)]
    greet(around(nx, ny, gx, gy) + [mate] + [(gx, 2 * b + core) for b in beside])

    def copy_to(at, source, place, device):
        return pltpu.make_async_remote_copy(
            src_ref=source, dst_ref=place, send_sem=ssend.at[at], recv_sem=srecv.at[at],
            device_id=device, device_id_type=MESH,
        )

    def run(copies):
        for copy in copies:
            copy.start()
        for copy in copies:
            copy.wait()

    border = border_copies(nx, ny, gx, gy, faces, halo, corners, send, recv)
    trade = trade_copies(nx, gx, gy, sending, coarse, tsend, trecv)
    first = copy_to(0, sums.at[at_rows((1 - core) * half, half)], pair_in, mate)
    first.start()
    start_border(border)
    for copy in trade:
        copy.start()
    keep_own(nx, gx, sending, coarse)
    first.wait()
    own = sums[at_rows(core * half, half)].astype(F32)
    pair_sum[...] = (own + pair_in[...].astype(F32)).astype(BF)
    run([
        copy_to(1 + k, pair_sum.at[at_rows(b * part, part)], line_in.at[k], (gx, 2 * b + core))
        for k, b in enumerate(beside)
    ])
    added = pair_sum[at_rows(line * part, part)].astype(F32)
    for k in range(lines - 1):
        added = added + line_in[k].astype(F32)
    line_sum[...] = added.astype(BF)
    base = lines
    run([
        copy_to(base + k, line_sum.at[at_rows(a * unit, unit)], row_in.at[k], (a, gy))
        for k, a in enumerate(along)
    ])
    added = line_sum[at_rows(gx * unit, unit)].astype(F32)
    for k in range(nx - 1):
        added = added + row_in[k].astype(F32)
    start = core * half + line * part
    mine = at_rows(start + gx * unit, unit)
    total[mine] = added.astype(BF)
    base = base + nx - 1
    run([copy_to(base + k, total.at[mine], total.at[mine], (a, gy)) for k, a in enumerate(along)])
    base = base + nx - 1
    mine = at_rows(start, part)
    run([
        copy_to(base + k, total.at[mine], total.at[mine], (gx, 2 * b + core))
        for k, b in enumerate(beside)
    ])
    base = base + lines - 1
    mine = at_rows(core * half, half)
    run([copy_to(base, total.at[mine], total.at[mine], mate)])
    wait_border(border)
    for copy in trade:
        copy.wait()


def swap_early(nx, ny, faces, cotangent):
    sems = [pltpu.SemaphoreType.DMA((8,))] * 2 + [pltpu.SemaphoreType.DMA((nx - 1,))] * 2
    return pl.pallas_call(
        functools.partial(early_kernel, nx, ny),
        out_shape=(
            jax.ShapeDtypeStruct((4, FACE, CH), BF),
            jax.ShapeDtypeStruct((4, SPAN, CH), BF),
            jax.ShapeDtypeStruct(cotangent.shape, BF),
        ),
        in_specs=[VM, VM],
        out_specs=(VM,) * 3,
        scratch_shapes=sems,
        compiler_params=pltpu.CompilerParams(
            collective_id=0, has_side_effects=True, vmem_limit_bytes=LIMIT
        ),
    )(faces, cotangent)


def swap_late(nx, ny, faces, sending, sums):
    rows = sums.shape[0]
    lines = ny // 2
    count = 2 * (1 + lines - 1 + nx - 1)
    sems = [pltpu.SemaphoreType.DMA((8,))] * 2 + [pltpu.SemaphoreType.DMA((nx - 1,))] * 2
    return pl.pallas_call(
        functools.partial(late_kernel, nx, ny),
        out_shape=(
            jax.ShapeDtypeStruct((4, FACE, CH), BF),
            jax.ShapeDtypeStruct((4, SPAN, CH), BF),
            jax.ShapeDtypeStruct(sending.shape, BF),
            jax.ShapeDtypeStruct(sums.shape, BF),
        ),
        in_specs=[VM] * 3,
        out_specs=(VM,) * 4,
        scratch_shapes=[
            pltpu.VMEM((rows // 2, CH), BF),
            pltpu.VMEM((lines - 1, rows // ny, CH), BF),
            pltpu.VMEM((nx - 1, rows // (nx * ny), CH), BF),
            pltpu.VMEM((rows // 2, CH), BF),
            pltpu.VMEM((rows // ny, CH), BF),
        ] + sems + [pltpu.SemaphoreType.DMA((count,))] * 2,
        compiler_params=pltpu.CompilerParams(
            collective_id=1, has_side_effects=True, vmem_limit_bytes=LIMIT
        ),
    )(faces, sending, sums)


def per_device(
    feats, voxel_mask, brick_coord, brick_count, route, conv_weight, down_weight, coarse_grad
):
    tiles_x = lax.axis_size("gx")
    tiles_y = lax.axis_size("gy")
    quarter = VOX // 8
    received = CAP * tiles_x
    params = pltpu.CompilerParams(vmem_limit_bytes=LIMIT)
    slot_ids = jnp.arange(SLOTS, dtype=jnp.int32)
    counts = brick_count[0, 0]
    occupied = jnp.where(slot_ids < BORDER, slot_ids < counts[0], slot_ids - BORDER < counts[1])
    mask = jnp.broadcast_to(
        jnp.where(occupied[:, None], voxel_mask[0, 0], 0).astype(BF)[:, :, None], (SLOTS, VOX, CH)
    )
    coord = brick_coord[0, 0]
    target = route[0, 0, :, 0] * CAP + route[0, 0, :, 1]
    feats = feats[0, 0]

    faces = pl.pallas_call(
        face_kernel,
        out_shape=jax.ShapeDtypeStruct((4, FACE, CH), BF),
        in_specs=[SM, VM, VM],
        out_specs=VM,
        scratch_shapes=[FACES],
        compiler_params=params,
    )(coord, feats, mask)
    halo, corners, returned = swap_early(
        tiles_x, tiles_y, faces, coarse_grad.reshape(received * quarter, CH)
    )
    returned = returned.reshape(received, quarter, CH)
    each = -(-35 * CH // (tiles_x * tiles_y))
    padded = -(-each // 16) * 16 * tiles_x * tiles_y
    order = pool_order()
    sending, grad_pre, grad_faces, sums = pl.pallas_call(
        main_kernel,
        out_shape=(
            jax.ShapeDtypeStruct((received, quarter, CH), BF),
            jax.ShapeDtypeStruct((SLOTS, VOX, CH), BF),
            jax.ShapeDtypeStruct((4, FACE, CH), BF),
            jax.ShapeDtypeStruct((padded, CH), BF),
        ),
        in_specs=[SM, SM] + [VM] * 9,
        out_specs=(VM,) * 4,
        scratch_shapes=[
            VOLUME, SHIFTED, COLUMNS, FACES,
            pltpu.VMEM((CH, 27 * CH), F32),
            pltpu.VMEM((SLOTS * quarter, CH), BF),
            pltpu.VMEM((SLOTS * quarter, 8 * CH), F32),
            pltpu.VMEM((SLOTS * quarter, 8 * CH), BF),
        ],
        compiler_params=params,
        cost_estimate=pl.CostEstimate(
            flops=4 * SLOTS * VOX * 27 * CH * CH, bytes_accessed=16 << 20, transcendentals=0
        ),
    )(
        coord, target, feats, mask, halo, corners, returned, conv_weight, down_weight,
        jnp.asarray(order, BF), jnp.asarray(order.T, BF),
    )
    grad_halo, grad_corners, coarse, total = swap_late(
        tiles_x, tiles_y, grad_faces, sending.reshape(received * quarter, CH), sums
    )
    coarse = coarse.reshape(1, 1, received, quarter, CH)
    flipped = conv_weight.reshape(27, CH, CH)[::-1].transpose(0, 2, 1).reshape(27 * CH, CH)
    feat_grad = pl.pallas_call(
        back_kernel,
        out_shape=jax.ShapeDtypeStruct((SLOTS, VOX, CH), BF),
        in_specs=[SM] + [VM] * 5,
        out_specs=VM,
        scratch_shapes=[VOLUME, SHIFTED, COLUMNS],
        compiler_params=params,
        cost_estimate=pl.CostEstimate(
            flops=2 * SLOTS * VOX * 27 * CH * CH, bytes_accessed=8 << 20, transcendentals=0
        ),
    )(coord, grad_pre, mask, grad_halo, grad_corners, flipped)
    total_slots = tiles_x * tiles_y * SLOTS
    conv_grad = total[: 27 * CH].astype(F32) * (1.0 / math.sqrt(total_slots * VOX))
    down_grad = total[27 * CH : 35 * CH].astype(F32) * (1.0 / math.sqrt(total_slots * VOX // 8))
    return (coarse, feat_grad[None, None], conv_grad, down_grad)


def solution(mesh):
    in_specs = (
        P("gx", "gy", None, None, None),
        P("gx", "gy", None, None),
        P("gx", "gy", None, None),
        P("gx", "gy", None),
        P("gx", "gy", None, None),
        P(),
        P(),
        P("gx", "gy", None, None, None),
    )
    out_specs = (P("gx", "gy", None, None, None), P("gx", "gy", None, None, None), P(), P())
    return jax.shard_map(
        per_device, mesh=mesh, in_specs=in_specs, out_specs=out_specs, check_vma=False
    )
```

```python
import functools
import math

import jax
import jax.numpy as jnp
from jax import lax
from jax.experimental import pallas as pl
from jax.experimental.pallas import tpu as pltpu
from jax.sharding import PartitionSpec as P

CH = 128
EDGE = 8
VOX = 512
TILE = 4
SLOTS = 16
BORDER = 8
CAP = 2
SPAN = TILE * EDGE
FACE = SPAN * SPAN
BF = jnp.bfloat16
F32 = jnp.float32
VM = pl.BlockSpec(memory_space=pltpu.VMEM)
SM = pl.BlockSpec(memory_space=pltpu.SMEM)
MESH = pl.DeviceIdType.MESH
LIMIT = 60 * 1024 * 1024


def half_rows(first, second):
    low = lax.broadcasted_iota(jnp.int32, first.shape, 1) < 4
    return (
        jnp.where(low, first, pltpu.roll(second, 4, 1)),
        jnp.where(low, pltpu.roll(first, 4, 1), second),
    )


def pool_rows(voxels):
    found = [None] * 8
    for pz in range(2):
        lines = voxels[pl.ds(pz, VOX // 2, stride=2), :].reshape(4, 2, 4, EDGE, CH)
        for px in range(2):
            pair = lines[:, px].reshape(EDGE, 2, EDGE, CH)
            for py, part in enumerate(half_rows(pair[:, 0], pair[:, 1])):
                found[4 * px + 2 * py + pz] = part.reshape(64, CH)
    return found


def unpool_rows(parts, voxels):
    for pz in range(2):
        planes = []
        for px in range(2):
            first = parts[4 * px + pz].reshape(EDGE, EDGE, CH)
            second = parts[4 * px + 2 + pz].reshape(EDGE, EDGE, CH)
            pair = jnp.stack(half_rows(first, second), axis=1)
            planes.append(pair.reshape(4, 4, EDGE, CH))
        lines = jnp.stack(planes, axis=1).reshape(VOX // 2, CH)
        voxels[pl.ds(pz, VOX // 2, stride=2), :] = lines


def put_faces(faces, cube, x, y, z):
    @pl.when(x == 0)
    def _():
        faces[0, pl.ds(y * EDGE, EDGE), z] = cube[0]

    @pl.when(x == TILE - 1)
    def _():
        faces[1, pl.ds(y * EDGE, EDGE), z] = cube[EDGE - 1]

    @pl.when(y == 0)
    def _():
        faces[2, pl.ds(x * EDGE, EDGE), z] = cube[:, 0]

    @pl.when(y == TILE - 1)
    def _():
        faces[3, pl.ds(x * EDGE, EDGE), z] = cube[:, EDGE - 1]


def face_kernel(coord, count, feats, voxel_mask, out, mask, faces, turned):
    faces[...] = jnp.zeros_like(faces)
    slot = lax.broadcasted_iota(jnp.int32, (SLOTS, VOX), 0)
    filled = slot < jnp.where(slot < BORDER, count[0], count[1] + BORDER)
    turned[...] = jnp.where(filled, voxel_mask[...], 0).astype(F32).T.astype(BF)

    def widen(s, carry):
        pick = lax.broadcasted_iota(jnp.int32, (SLOTS, CH), 0) == s
        mask[s] = jnp.dot(
            turned[...], pick.astype(F32).astype(BF), preferred_element_type=F32
        ).astype(BF)
        return carry

    lax.fori_loop(0, SLOTS, widen, 0)

    def body(s, carry):
        cube = (feats[s].astype(F32) * mask[s].astype(F32)).reshape(EDGE, EDGE, EDGE, CH)
        put_faces(faces, cube, coord[s, 0], coord[s, 1], coord[s, 2])
        return carry

    lax.fori_loop(0, BORDER, body, 0)
    out[...] = faces[...].reshape(4, FACE, CH).astype(BF)


def fill_volume(volume, halo, corners):
    def clear(i, carry):
        volume[i] = jnp.zeros(volume.shape[1:], F32)
        return carry

    lax.fori_loop(0, volume.shape[0], clear, 0)
    inner = slice(1, 1 + SPAN)
    depth = slice(1, 1 + TILE)
    plane = (SPAN, TILE, EDGE, CH)
    volume[0, inner, depth] = halo[0].astype(F32).reshape(plane)
    volume[1 + SPAN, inner, depth] = halo[1].astype(F32).reshape(plane)
    volume[inner, 0, depth] = halo[2].astype(F32).reshape(plane)
    volume[inner, 1 + SPAN, depth] = halo[3].astype(F32).reshape(plane)
    for at, (cx, cy) in enumerate(((0, 0), (0, 1), (1, 0), (1, 1))):
        line = corners[at].astype(F32).reshape(TILE, EDGE, CH)
        volume[cx * (1 + SPAN), cy * (1 + SPAN), depth] = line


def place_brick(volume, cube, x, y, z):
    volume[pl.ds(1 + x * EDGE, EDGE), pl.ds(1 + y * EDGE, EDGE), 1 + z] = cube


def unfold(volume, shifted, columns, x, y, z):
    ys = pl.ds(y * EDGE, EDGE + 2)
    row = lax.broadcasted_iota(jnp.int32, (EDGE, CH), 0)[None]

    def lines(i, carry):
        at = x * EDGE + i
        mid = volume[at, ys, z + 1]
        low = jnp.where(row == EDGE - 1, volume[at, ys, z], mid)
        high = jnp.where(row == 0, volume[at, ys, z + 2], mid)
        shifted[0, i] = pltpu.roll(low, 1, 1)
        shifted[1, i] = mid
        shifted[2, i] = pltpu.roll(high, EDGE - 1, 1)
        return carry

    lax.fori_loop(0, EDGE + 2, lines, 0, unroll=True)
    for tap in range(27):
        a, b, c = tap // 9, tap // 3 % 3, tap % 3
        piece = shifted[c, a : a + EDGE, b : b + EDGE].reshape(VOX, CH).astype(BF)
        columns[:, tap * CH : (tap + 1) * CH] = piece


def main_kernel(
    coord, target, feats, mask, halo, corners, returned, weight, down,
    sending, grad_out, face_out, sums,
    volume, shifted_a, columns_a, shifted_b, columns_b, faces, conv_acc, grads, back_rows,
    blocks, voxels_a, voxels_b,
):
    fill_volume(volume, halo, corners)
    faces[...] = jnp.zeros_like(faces)
    conv_acc[...] = jnp.zeros_like(conv_acc)
    sending[...] = jnp.zeros_like(sending)

    def place(s, carry):
        cube = (feats[s].astype(F32) * mask[s].astype(F32)).reshape(EDGE, EDGE, EDGE, CH)
        place_brick(volume, cube, coord[s, 0], coord[s, 1], coord[s, 2])
        rows = pl.ds(pl.multiple_of(s * 64, 64), 64)
        grads[rows] = returned[target[s]]
        return carry

    lax.fori_loop(0, SLOTS, place, 0)

    def spread(i, carry):
        rows = pl.ds(pl.multiple_of(i * 256, 256), 256)
        back_rows[rows] = lax.dot_general(
            grads[rows], down[...], (((1,), (1,)), ((), ())), preferred_element_type=F32
        )
        return carry

    lax.fori_loop(0, SLOTS // 4, spread, 0)

    def local(s, columns, voxels):
        rows = pl.ds(pl.multiple_of(s * 64, 64), 64)
        preact = jnp.dot(columns[...], weight[...], preferred_element_type=F32)
        active = mask[s].astype(F32)
        sig = jax.nn.sigmoid(preact)
        voxels[...] = preact * sig * active
        blocks[rows] = jnp.concatenate([p.astype(BF) for p in pool_rows(voxels)], axis=1)
        wide = back_rows[rows]
        unpool_rows([wide[:, CH * q : CH * q + CH] for q in range(8)], voxels)
        grad = (voxels[...] * active * sig * (1.0 + preact * (1.0 - sig))).astype(BF)
        grad_out[s] = grad
        return grad.astype(F32).T.astype(BF)

    def body(i, carry):
        s, t = 2 * i, 2 * i + 1
        unfold(volume, shifted_a, columns_a, coord[s, 0], coord[s, 1], coord[s, 2])
        unfold(volume, shifted_b, columns_b, coord[t, 0], coord[t, 1], coord[t, 2])
        first = local(s, columns_a, voxels_a)
        second = local(t, columns_b, voxels_b)
        conv_acc[...] += jnp.dot(first, columns_a[...], preferred_element_type=F32) + jnp.dot(
            second, columns_b[...], preferred_element_type=F32
        )
        return carry

    lax.fori_loop(0, SLOTS // 2, body, 0)

    def edge(s, carry):
        cube = grad_out[s].astype(F32).reshape(EDGE, EDGE, EDGE, CH)
        put_faces(faces, cube, coord[s, 0], coord[s, 1], coord[s, 2])
        return carry

    lax.fori_loop(0, BORDER, edge, 0)
    face_out[...] = faces[...].reshape(4, FACE, CH).astype(BF)
    for tap in range(27):
        sums[tap * CH : (tap + 1) * CH] = conv_acc[:, tap * CH : (tap + 1) * CH].T
    turned = grads[...].astype(F32).T.astype(BF)
    down_acc = jnp.dot(turned, blocks[...], preferred_element_type=F32)
    for q in range(8):
        rows = slice((27 + q) * CH, (28 + q) * CH)
        sums[rows] = down_acc[:, q * CH : (q + 1) * CH].T
    if sums.shape[0] > 35 * CH:
        sums[35 * CH :] = jnp.zeros((sums.shape[0] - 35 * CH, CH), F32)

    def send(s, carry):
        rows = pl.ds(pl.multiple_of(s * 64, 64), 64)
        sub = jnp.dot(blocks[rows], down[...], preferred_element_type=F32)
        sending[target[s]] = sub.astype(BF)
        return carry

    lax.fori_loop(0, SLOTS, send, 0)


def back_kernel(
    coord, grad, mask, halo, corners, weight, out,
    volume, shifted_a, columns_a, shifted_b, columns_b, flipped,
):
    fill_volume(volume, halo, corners)
    for tap in range(27):
        block = weight[(26 - tap) * CH : (27 - tap) * CH].astype(F32)
        flipped[tap * CH : (tap + 1) * CH] = block.T.astype(BF)

    def place(s, carry):
        cube = grad[s].astype(F32).reshape(EDGE, EDGE, EDGE, CH)
        place_brick(volume, cube, coord[s, 0], coord[s, 1], coord[s, 2])
        return carry

    lax.fori_loop(0, SLOTS, place, 0)

    def body(i, carry):
        s, t = 2 * i, 2 * i + 1
        unfold(volume, shifted_a, columns_a, coord[s, 0], coord[s, 1], coord[s, 2])
        unfold(volume, shifted_b, columns_b, coord[t, 0], coord[t, 1], coord[t, 2])
        for slot, columns in ((s, columns_a), (t, columns_b)):
            back = jnp.dot(columns[...], flipped[...], preferred_element_type=F32)
            out[slot] = (back * mask[slot].astype(F32)).astype(BF)
        return carry

    lax.fori_loop(0, SLOTS // 2, body, 0)


VOLUME = pltpu.VMEM((SPAN + 2, SPAN + 2, TILE + 2, EDGE, CH), F32)
SHIFTED = pltpu.VMEM((3, EDGE + 2, EDGE + 2, EDGE, CH), F32)
COLUMNS = pltpu.VMEM((VOX, 27 * CH), BF)
PAIR = [SHIFTED, COLUMNS, SHIFTED, COLUMNS]
FACES = pltpu.VMEM((4, SPAN, TILE, EDGE, CH), F32)


def at_rows(start, size):
    return pl.ds(pl.multiple_of(start, 16), size)


def greet(peers):
    barrier = pltpu.get_barrier_semaphore()
    for peer in peers:
        pl.semaphore_signal(barrier, inc=1, device_id=peer, device_id_type=MESH)
    pl.semaphore_wait(barrier, len(peers))


def around(nx, ny, gx, gy):
    ring = [
        (lax.rem(gx + dx + nx, nx), lax.rem(gy + dy + ny, ny))
        for dx in (-1, 0, 1)
        for dy in (-1, 0, 1)
        if dx or dy
    ]
    return ring + [(lax.rem(gx + k, nx), gy) for k in range(1, nx)]


def border_copies(nx, ny, gx, gy, faces, halo, corners, send, recv):
    plan = [
        (1, 0, faces.at[1], halo.at[0]),
        (-1, 0, faces.at[0], halo.at[1]),
        (0, 1, faces.at[3], halo.at[2]),
        (0, -1, faces.at[2], halo.at[3]),
    ]
    for at, (cx, cy) in enumerate(((0, 0), (0, 1), (1, 0), (1, 1))):
        rows = pl.ds(FACE - SPAN if cy == 0 else 0, SPAN)
        plan.append((1 - 2 * cx, 1 - 2 * cy, faces.at[1 - cx, rows], corners.at[at]))
    copies = []
    for at, (dx, dy, source, place) in enumerate(plan):
        sends = (gx + dx >= 0) & (gx + dx < nx) & (gy + dy >= 0) & (gy + dy < ny)
        gets = (gx - dx >= 0) & (gx - dx < nx) & (gy - dy >= 0) & (gy - dy < ny)
        copy = pltpu.make_async_remote_copy(
            src_ref=source, dst_ref=place, send_sem=send.at[at], recv_sem=recv.at[at],
            device_id=(lax.rem(gx + dx + nx, nx), lax.rem(gy + dy + ny, ny)),
            device_id_type=MESH,
        )
        copies.append((copy, place, sends, gets))
    return copies


def start_border(copies):
    for copy, place, sends, gets in copies:

        @pl.when(sends)
        def _(copy=copy):
            copy.start()

        @pl.when(jnp.logical_not(gets))
        def _(place=place):
            place[...] = jnp.zeros(place.shape, BF)


def wait_border(copies):
    for copy, place, sends, gets in copies:

        @pl.when(sends)
        def _(copy=copy):
            copy.wait_send()

        @pl.when(gets)
        def _(copy=copy):
            copy.wait_recv()


def trade_copies(nx, gx, gy, source, place, send, recv):
    block = source.shape[0] // nx
    copies = []
    for k in range(1, nx):
        peer = lax.rem(gx + k, nx)
        copies.append(
            pltpu.make_async_remote_copy(
                src_ref=source.at[at_rows(peer * block, block)],
                dst_ref=place.at[at_rows(gx * block, block)],
                send_sem=send.at[k - 1], recv_sem=recv.at[k - 1],
                device_id=(peer, gy), device_id_type=MESH,
            )
        )
    return copies


def keep_own(nx, gx, source, place):
    block = source.shape[0] // nx
    place[at_rows(gx * block, block)] = source[at_rows(gx * block, block)]


def early_kernel(nx, ny, faces, cotangent, halo, corners, returned, send, recv, tsend, trecv):
    gx, gy = lax.axis_index("gx"), lax.axis_index("gy")
    greet(around(nx, ny, gx, gy))
    border = border_copies(nx, ny, gx, gy, faces, halo, corners, send, recv)
    trade = trade_copies(nx, gx, gy, cotangent, returned, tsend, trecv)
    start_border(border)
    for copy in trade:
        copy.start()
    keep_own(nx, gx, cotangent, returned)
    wait_border(border)
    for copy in trade:
        copy.wait()


def late_kernel(
    nx, ny, faces, sending, sums, halo, corners, coarse, total,
    pair_in, line_in, row_in, pair_out, pair_sum, pair_send, line_sum, line_send, send, recv, tsend, trecv, ssend, srecv,
):
    gx, gy = lax.axis_index("gx"), lax.axis_index("gy")
    core, line, lines = lax.rem(gy, 2), gy // 2, ny // 2
    half = sums.shape[0] // 2
    part = half // lines
    unit = part // nx
    mate = (gx, gy + 1 - 2 * core)
    beside = [lax.rem(line + k, lines) for k in range(1, lines)]
    along = [lax.rem(gx + k, nx) for k in range(1, nx)]
    greet(around(nx, ny, gx, gy) + [mate] + [(gx, 2 * b + core) for b in beside])

    def copy_to(at, source, place, device):
        return pltpu.make_async_remote_copy(
            src_ref=source, dst_ref=place, send_sem=ssend.at[at], recv_sem=srecv.at[at],
            device_id=device, device_id_type=MESH,
        )

    def run(copies):
        for copy in copies:
            copy.start()
        for copy in copies:
            copy.wait()

    border = border_copies(nx, ny, gx, gy, faces, halo, corners, send, recv)
    trade = trade_copies(nx, gx, gy, sending, coarse, tsend, trecv)
    pair_out[...] = sums[at_rows((1 - core) * half, half)].astype(BF)
    first = copy_to(0, pair_out, pair_in, mate)
    first.start()
    start_border(border)
    for copy in trade:
        copy.start()
    keep_own(nx, gx, sending, coarse)
    first.wait()
    pair_sum[...] = sums[at_rows(core * half, half)] + pair_in[...].astype(F32)
    pair_send[...] = pair_sum[...].astype(BF)
    run([
        copy_to(1 + k, pair_send.at[at_rows(b * part, part)], line_in.at[k], (gx, 2 * b + core))
        for k, b in enumerate(beside)
    ])
    added = pair_sum[at_rows(line * part, part)]
    for k in range(lines - 1):
        added = added + line_in[k].astype(F32)
    line_sum[...] = added
    line_send[...] = added.astype(BF)
    base = lines
    run([
        copy_to(base + k, line_send.at[at_rows(a * unit, unit)], row_in.at[k], (a, gy))
        for k, a in enumerate(along)
    ])
    added = line_sum[at_rows(gx * unit, unit)]
    for k in range(nx - 1):
        added = added + row_in[k].astype(F32)
    start = core * half + line * part
    mine = at_rows(start + gx * unit, unit)
    total[mine] = added.astype(BF)
    base = base + nx - 1
    run([copy_to(base + k, total.at[mine], total.at[mine], (a, gy)) for k, a in enumerate(along)])
    base = base + nx - 1
    mine = at_rows(start, part)
    run([
        copy_to(base + k, total.at[mine], total.at[mine], (gx, 2 * b + core))
        for k, b in enumerate(beside)
    ])
    base = base + lines - 1
    mine = at_rows(core * half, half)
    run([copy_to(base, total.at[mine], total.at[mine], mate)])
    wait_border(border)
    for copy in trade:
        copy.wait()


def swap_early(nx, ny, faces, cotangent):
    sems = [pltpu.SemaphoreType.DMA((8,))] * 2 + [pltpu.SemaphoreType.DMA((nx - 1,))] * 2
    return pl.pallas_call(
        functools.partial(early_kernel, nx, ny),
        out_shape=(
            jax.ShapeDtypeStruct((4, FACE, CH), BF),
            jax.ShapeDtypeStruct((4, SPAN, CH), BF),
            jax.ShapeDtypeStruct(cotangent.shape, BF),
        ),
        in_specs=[VM, VM],
        out_specs=(VM,) * 3,
        scratch_shapes=sems,
        compiler_params=pltpu.CompilerParams(
            collective_id=0, has_side_effects=True, vmem_limit_bytes=LIMIT
        ),
    )(faces, cotangent)


def swap_late(nx, ny, faces, sending, sums):
    rows = sums.shape[0]
    lines = ny // 2
    count = 2 * (1 + lines - 1 + nx - 1)
    sems = [pltpu.SemaphoreType.DMA((8,))] * 2 + [pltpu.SemaphoreType.DMA((nx - 1,))] * 2
    return pl.pallas_call(
        functools.partial(late_kernel, nx, ny),
        out_shape=(
            jax.ShapeDtypeStruct((4, FACE, CH), BF),
            jax.ShapeDtypeStruct((4, SPAN, CH), BF),
            jax.ShapeDtypeStruct(sending.shape, BF),
            jax.ShapeDtypeStruct(sums.shape, BF),
        ),
        in_specs=[VM] * 3,
        out_specs=(VM,) * 4,
        scratch_shapes=[
            pltpu.VMEM((rows // 2, CH), BF),
            pltpu.VMEM((lines - 1, rows // ny, CH), BF),
            pltpu.VMEM((nx - 1, rows // (nx * ny), CH), BF),
            pltpu.VMEM((rows // 2, CH), BF),
            pltpu.VMEM((rows // 2, CH), F32),
            pltpu.VMEM((rows // 2, CH), BF),
            pltpu.VMEM((rows // ny, CH), F32),
            pltpu.VMEM((rows // ny, CH), BF),
        ] + sems + [pltpu.SemaphoreType.DMA((count,))] * 2,
        compiler_params=pltpu.CompilerParams(
            collective_id=1, has_side_effects=True, vmem_limit_bytes=LIMIT
        ),
    )(faces, sending, sums)


def per_device(
    feats, voxel_mask, brick_coord, brick_count, route, conv_weight, down_weight, coarse_grad
):
    tiles_x = lax.axis_size("gx")
    tiles_y = lax.axis_size("gy")
    quarter = VOX // 8
    received = CAP * tiles_x
    params = pltpu.CompilerParams(vmem_limit_bytes=LIMIT)
    coord = brick_coord[0, 0]
    target = route[0, 0, :, 0] * CAP + route[0, 0, :, 1]
    feats = feats[0, 0]

    faces, mask = pl.pallas_call(
        face_kernel,
        out_shape=(
            jax.ShapeDtypeStruct((4, FACE, CH), BF),
            jax.ShapeDtypeStruct((SLOTS, VOX, CH), BF),
        ),
        in_specs=[SM, SM, VM, VM],
        out_specs=(VM, VM),
        scratch_shapes=[FACES, pltpu.VMEM((VOX, SLOTS), BF)],
        compiler_params=params,
    )(coord, brick_count[0, 0], feats, voxel_mask[0, 0])
    halo, corners, returned = swap_early(
        tiles_x, tiles_y, faces, coarse_grad.reshape(received * quarter, CH)
    )
    returned = returned.reshape(received, quarter, CH)
    each = -(-35 * CH // (tiles_x * tiles_y))
    padded = -(-each // 16) * 16 * tiles_x * tiles_y
    sending, grad_pre, grad_faces, sums = pl.pallas_call(
        main_kernel,
        out_shape=(
            jax.ShapeDtypeStruct((received, quarter, CH), BF),
            jax.ShapeDtypeStruct((SLOTS, VOX, CH), BF),
            jax.ShapeDtypeStruct((4, FACE, CH), BF),
            jax.ShapeDtypeStruct((padded, CH), F32),
        ),
        in_specs=[SM, SM] + [VM] * 7,
        out_specs=(VM,) * 4,
        scratch_shapes=[
            VOLUME, *PAIR, FACES,
            pltpu.VMEM((CH, 27 * CH), F32),
            pltpu.VMEM((SLOTS * quarter, CH), BF),
            pltpu.VMEM((SLOTS * quarter, 8 * CH), F32),
            pltpu.VMEM((SLOTS * quarter, 8 * CH), BF),
            pltpu.VMEM((VOX, CH), F32),
            pltpu.VMEM((VOX, CH), F32),
        ],
        compiler_params=params,
        cost_estimate=pl.CostEstimate(
            flops=4 * SLOTS * VOX * 27 * CH * CH, bytes_accessed=16 << 20, transcendentals=0
        ),
    )(
        coord, target, feats, mask, halo, corners, returned, conv_weight, down_weight,
    )
    grad_halo, grad_corners, coarse, total = swap_late(
        tiles_x, tiles_y, grad_faces, sending.reshape(received * quarter, CH), sums
    )
    coarse = coarse.reshape(1, 1, received, quarter, CH)
    feat_grad = pl.pallas_call(
        back_kernel,
        out_shape=jax.ShapeDtypeStruct((SLOTS, VOX, CH), BF),
        in_specs=[SM] + [VM] * 5,
        out_specs=VM,
        scratch_shapes=[VOLUME, *PAIR, pltpu.VMEM((27 * CH, CH), BF)],
        compiler_params=params,
        cost_estimate=pl.CostEstimate(
            flops=2 * SLOTS * VOX * 27 * CH * CH, bytes_accessed=8 << 20, transcendentals=0
        ),
    )(coord, grad_pre, mask, grad_halo, grad_corners, conv_weight)
    total_slots = tiles_x * tiles_y * SLOTS
    conv_grad = total[: 27 * CH].astype(F32) * (1.0 / math.sqrt(total_slots * VOX))
    down_grad = total[27 * CH : 35 * CH].astype(F32) * (1.0 / math.sqrt(total_slots * VOX // 8))
    return (coarse, feat_grad[None, None], conv_grad, down_grad)


def solution(mesh):
    in_specs = (
        P("gx", "gy", None, None, None),
        P("gx", "gy", None, None),
        P("gx", "gy", None, None),
        P("gx", "gy", None),
        P("gx", "gy", None, None),
        P(),
        P(),
        P("gx", "gy", None, None, None),
    )
    out_specs = (P("gx", "gy", None, None, None), P("gx", "gy", None, None, None), P(), P())
    return jax.shard_map(
        per_device, mesh=mesh, in_specs=in_specs, out_specs=out_specs, check_vma=False
    )
```

```python
import functools
import math

import jax
import jax.numpy as jnp
from jax import lax
from jax.experimental import pallas as pl
from jax.experimental.pallas import tpu as pltpu
from jax.sharding import PartitionSpec as P

CH = 128
EDGE = 8
VOX = 512
TILE = 4
SLOTS = 16
BORDER = 8
CAP = 2
SPAN = TILE * EDGE
FACE = SPAN * SPAN
BF = jnp.bfloat16
F32 = jnp.float32
VM = pl.BlockSpec(memory_space=pltpu.VMEM)
SM = pl.BlockSpec(memory_space=pltpu.SMEM)
MESH = pl.DeviceIdType.MESH
LIMIT = 60 * 1024 * 1024


def half_rows(first, second):
    low = lax.broadcasted_iota(jnp.int32, first.shape, 1) < 4
    return (
        jnp.where(low, first, pltpu.roll(second, 4, 1)),
        jnp.where(low, pltpu.roll(first, 4, 1), second),
    )


def pool_rows(voxels):
    found = [None] * 8
    for pz in range(2):
        lines = voxels[pl.ds(pz, VOX // 2, stride=2), :].reshape(4, 2, 4, EDGE, CH)
        for px in range(2):
            pair = lines[:, px].reshape(EDGE, 2, EDGE, CH)
            for py, part in enumerate(half_rows(pair[:, 0], pair[:, 1])):
                found[4 * px + 2 * py + pz] = part.reshape(64, CH)
    return found


def unpool_rows(parts, voxels):
    for pz in range(2):
        planes = []
        for px in range(2):
            first = parts[4 * px + pz].reshape(EDGE, EDGE, CH)
            second = parts[4 * px + 2 + pz].reshape(EDGE, EDGE, CH)
            pair = jnp.stack(half_rows(first, second), axis=1)
            planes.append(pair.reshape(4, 4, EDGE, CH))
        lines = jnp.stack(planes, axis=1).reshape(VOX // 2, CH)
        voxels[pl.ds(pz, VOX // 2, stride=2), :] = lines


def put_faces(faces, cube, x, y, z):
    @pl.when(x == 0)
    def _():
        faces[0, pl.ds(y * EDGE, EDGE), z] = cube[0]

    @pl.when(x == TILE - 1)
    def _():
        faces[1, pl.ds(y * EDGE, EDGE), z] = cube[EDGE - 1]

    @pl.when(y == 0)
    def _():
        faces[2, pl.ds(x * EDGE, EDGE), z] = cube[:, 0]

    @pl.when(y == TILE - 1)
    def _():
        faces[3, pl.ds(x * EDGE, EDGE), z] = cube[:, EDGE - 1]


def face_kernel(coord, count, feats, voxel_mask, out, mask, faces, turned):
    faces[...] = jnp.zeros_like(faces)
    slot = lax.broadcasted_iota(jnp.int32, (SLOTS, VOX), 0)
    filled = slot < jnp.where(slot < BORDER, count[0], count[1] + BORDER)
    turned[...] = jnp.where(filled, voxel_mask[...], 0).astype(F32).T.astype(BF)

    def widen(s, carry):
        pick = lax.broadcasted_iota(jnp.int32, (SLOTS, CH), 0) == s
        mask[s] = jnp.dot(
            turned[...], pick.astype(F32).astype(BF), preferred_element_type=F32
        ).astype(BF)
        return carry

    lax.fori_loop(0, SLOTS, widen, 0)

    def body(s, carry):
        cube = (feats[s].astype(F32) * mask[s].astype(F32)).reshape(EDGE, EDGE, EDGE, CH)
        put_faces(faces, cube, coord[s, 0], coord[s, 1], coord[s, 2])
        return carry

    lax.fori_loop(0, BORDER, body, 0)
    out[...] = faces[...].reshape(4, FACE, CH).astype(BF)


def fill_volume(volume, halo, corners):
    def clear(i, carry):
        volume[i] = jnp.zeros(volume.shape[1:], F32)
        return carry

    lax.fori_loop(0, volume.shape[0], clear, 0)
    inner = slice(1, 1 + SPAN)
    depth = slice(1, 1 + TILE)
    plane = (SPAN, TILE, EDGE, CH)
    volume[0, inner, depth] = halo[0].astype(F32).reshape(plane)
    volume[1 + SPAN, inner, depth] = halo[1].astype(F32).reshape(plane)
    volume[inner, 0, depth] = halo[2].astype(F32).reshape(plane)
    volume[inner, 1 + SPAN, depth] = halo[3].astype(F32).reshape(plane)
    for at, (cx, cy) in enumerate(((0, 0), (0, 1), (1, 0), (1, 1))):
        line = corners[at].astype(F32).reshape(TILE, EDGE, CH)
        volume[cx * (1 + SPAN), cy * (1 + SPAN), depth] = line


def place_brick(volume, cube, x, y, z):
    volume[pl.ds(1 + x * EDGE, EDGE), pl.ds(1 + y * EDGE, EDGE), 1 + z] = cube


def unfold(volume, shifted, columns, x, y, z):
    ys = pl.ds(y * EDGE, EDGE + 2)
    row = lax.broadcasted_iota(jnp.int32, (EDGE, CH), 0)[None]

    def lines(i, carry):
        at = x * EDGE + i
        mid = volume[at, ys, z + 1]
        low = jnp.where(row == EDGE - 1, volume[at, ys, z], mid)
        high = jnp.where(row == 0, volume[at, ys, z + 2], mid)
        shifted[0, i] = pltpu.roll(low, 1, 1)
        shifted[1, i] = mid
        shifted[2, i] = pltpu.roll(high, EDGE - 1, 1)
        return carry

    lax.fori_loop(0, EDGE + 2, lines, 0, unroll=True)
    for tap in range(27):
        a, b, c = tap // 9, tap // 3 % 3, tap % 3
        piece = shifted[c, a : a + EDGE, b : b + EDGE].reshape(VOX, CH).astype(BF)
        columns[:, tap * CH : (tap + 1) * CH] = piece


def main_kernel(
    coord, target, feats, mask, halo, corners, returned, weight, down,
    sending, grad_out, face_out, sums,
    volume, shifted_a, columns_a, shifted_b, columns_b, faces, conv_acc, grads, back_rows,
    blocks, voxels_a, voxels_b,
):
    fill_volume(volume, halo, corners)
    faces[...] = jnp.zeros_like(faces)
    conv_acc[...] = jnp.zeros_like(conv_acc)
    sending[...] = jnp.zeros_like(sending)

    def place(s, carry):
        cube = (feats[s].astype(F32) * mask[s].astype(F32)).reshape(EDGE, EDGE, EDGE, CH)
        place_brick(volume, cube, coord[s, 0], coord[s, 1], coord[s, 2])
        rows = pl.ds(pl.multiple_of(s * 64, 64), 64)
        grads[rows] = returned[target[s]]
        return carry

    lax.fori_loop(0, SLOTS, place, 0)

    def spread(i, carry):
        rows = pl.ds(pl.multiple_of(i * 256, 256), 256)
        back_rows[rows] = lax.dot_general(
            grads[rows], down[...], (((1,), (1,)), ((), ())), preferred_element_type=F32
        )
        return carry

    lax.fori_loop(0, SLOTS // 4, spread, 0)

    def local(s, columns, voxels):
        rows = pl.ds(pl.multiple_of(s * 64, 64), 64)
        preact = jnp.dot(columns[...], weight[...], preferred_element_type=F32)
        active = mask[s].astype(F32)
        sig = jax.nn.sigmoid(preact)
        voxels[...] = preact * sig * active
        blocks[rows] = jnp.concatenate([p.astype(BF) for p in pool_rows(voxels)], axis=1)
        wide = back_rows[rows]
        unpool_rows([wide[:, CH * q : CH * q + CH] for q in range(8)], voxels)
        grad = (voxels[...] * active * sig * (1.0 + preact * (1.0 - sig))).astype(BF)
        grad_out[s] = grad
        return grad.astype(F32).T.astype(BF)

    def body(i, carry):
        s, t = 2 * i, 2 * i + 1
        unfold(volume, shifted_a, columns_a, coord[s, 0], coord[s, 1], coord[s, 2])
        unfold(volume, shifted_b, columns_b, coord[t, 0], coord[t, 1], coord[t, 2])
        first = local(s, columns_a, voxels_a)
        second = local(t, columns_b, voxels_b)
        conv_acc[...] += jnp.dot(first, columns_a[...], preferred_element_type=F32) + jnp.dot(
            second, columns_b[...], preferred_element_type=F32
        )
        return carry

    lax.fori_loop(0, SLOTS // 2, body, 0)

    def edge(s, carry):
        cube = grad_out[s].astype(F32).reshape(EDGE, EDGE, EDGE, CH)
        put_faces(faces, cube, coord[s, 0], coord[s, 1], coord[s, 2])
        return carry

    lax.fori_loop(0, BORDER, edge, 0)
    face_out[...] = faces[...].reshape(4, FACE, CH).astype(BF)
    for tap in range(27):
        sums[tap * CH : (tap + 1) * CH] = conv_acc[:, tap * CH : (tap + 1) * CH].T
    turned = grads[...].astype(F32).T.astype(BF)
    down_acc = jnp.dot(turned, blocks[...], preferred_element_type=F32)
    for q in range(8):
        rows = slice((27 + q) * CH, (28 + q) * CH)
        sums[rows] = down_acc[:, q * CH : (q + 1) * CH].T
    if sums.shape[0] > 35 * CH:
        sums[35 * CH :] = jnp.zeros((sums.shape[0] - 35 * CH, CH), F32)

    def send(s, carry):
        rows = pl.ds(pl.multiple_of(s * 64, 64), 64)
        sub = jnp.dot(blocks[rows], down[...], preferred_element_type=F32)
        sending[target[s]] = sub.astype(BF)
        return carry

    lax.fori_loop(0, SLOTS, send, 0)


def back_kernel(
    coord, grad, mask, halo, corners, weight, out,
    volume, shifted_a, columns_a, shifted_b, columns_b, flipped,
):
    fill_volume(volume, halo, corners)
    for tap in range(27):
        block = weight[(26 - tap) * CH : (27 - tap) * CH].astype(F32)
        flipped[tap * CH : (tap + 1) * CH] = block.T.astype(BF)

    def place(s, carry):
        cube = grad[s].astype(F32).reshape(EDGE, EDGE, EDGE, CH)
        place_brick(volume, cube, coord[s, 0], coord[s, 1], coord[s, 2])
        return carry

    lax.fori_loop(0, SLOTS, place, 0)

    def body(i, carry):
        s, t = 2 * i, 2 * i + 1
        unfold(volume, shifted_a, columns_a, coord[s, 0], coord[s, 1], coord[s, 2])
        unfold(volume, shifted_b, columns_b, coord[t, 0], coord[t, 1], coord[t, 2])
        for slot, columns in ((s, columns_a), (t, columns_b)):
            back = jnp.dot(columns[...], flipped[...], preferred_element_type=F32)
            out[slot] = (back * mask[slot].astype(F32)).astype(BF)
        return carry

    lax.fori_loop(0, SLOTS // 2, body, 0)


VOLUME = pltpu.VMEM((SPAN + 2, SPAN + 2, TILE + 2, EDGE, CH), F32)
SHIFTED = pltpu.VMEM((3, EDGE + 2, EDGE + 2, EDGE, CH), F32)
COLUMNS = pltpu.VMEM((VOX, 27 * CH), BF)
PAIR = [SHIFTED, COLUMNS, SHIFTED, COLUMNS]
FACES = pltpu.VMEM((4, SPAN, TILE, EDGE, CH), F32)


def at_rows(start, size):
    return pl.ds(pl.multiple_of(start, 16), size)


def greet(peers):
    barrier = pltpu.get_barrier_semaphore()
    for peer in peers:
        pl.semaphore_signal(barrier, inc=1, device_id=peer, device_id_type=MESH)
    pl.semaphore_wait(barrier, len(peers))


def around(nx, ny, gx, gy):
    ring = [
        (lax.rem(gx + dx + nx, nx), lax.rem(gy + dy + ny, ny))
        for dx in (-1, 0, 1)
        for dy in (-1, 0, 1)
        if dx or dy
    ]
    return ring + [(lax.rem(gx + k, nx), gy) for k in range(1, nx)]


def border_copies(nx, ny, gx, gy, faces, halo, corners, send, recv):
    plan = [
        (1, 0, faces.at[1], halo.at[0]),
        (-1, 0, faces.at[0], halo.at[1]),
        (0, 1, faces.at[3], halo.at[2]),
        (0, -1, faces.at[2], halo.at[3]),
    ]
    for at, (cx, cy) in enumerate(((0, 0), (0, 1), (1, 0), (1, 1))):
        rows = pl.ds(FACE - SPAN if cy == 0 else 0, SPAN)
        plan.append((1 - 2 * cx, 1 - 2 * cy, faces.at[1 - cx, rows], corners.at[at]))
    copies = []
    for at, (dx, dy, source, place) in enumerate(plan):
        sends = (gx + dx >= 0) & (gx + dx < nx) & (gy + dy >= 0) & (gy + dy < ny)
        gets = (gx - dx >= 0) & (gx - dx < nx) & (gy - dy >= 0) & (gy - dy < ny)
        copy = pltpu.make_async_remote_copy(
            src_ref=source, dst_ref=place, send_sem=send.at[at], recv_sem=recv.at[at],
            device_id=(lax.rem(gx + dx + nx, nx), lax.rem(gy + dy + ny, ny)),
            device_id_type=MESH,
        )
        copies.append((copy, place, sends, gets))
    return copies


def start_border(copies):
    for copy, place, sends, gets in copies:

        @pl.when(sends)
        def _(copy=copy):
            copy.start()

        @pl.when(jnp.logical_not(gets))
        def _(place=place):
            place[...] = jnp.zeros(place.shape, BF)


def wait_border(copies):
    for copy, place, sends, gets in copies:

        @pl.when(sends)
        def _(copy=copy):
            copy.wait_send()

        @pl.when(gets)
        def _(copy=copy):
            copy.wait_recv()


def trade_copies(nx, gx, gy, source, place, send, recv):
    block = source.shape[0] // nx
    copies = []
    for k in range(1, nx):
        peer = lax.rem(gx + k, nx)
        copies.append(
            pltpu.make_async_remote_copy(
                src_ref=source.at[at_rows(peer * block, block)],
                dst_ref=place.at[at_rows(gx * block, block)],
                send_sem=send.at[k - 1], recv_sem=recv.at[k - 1],
                device_id=(peer, gy), device_id_type=MESH,
            )
        )
    return copies


def keep_own(nx, gx, source, place):
    block = source.shape[0] // nx
    place[at_rows(gx * block, block)] = source[at_rows(gx * block, block)]


def early_kernel(nx, ny, faces, cotangent, halo, corners, returned, send, recv, tsend, trecv):
    gx, gy = lax.axis_index("gx"), lax.axis_index("gy")
    greet(around(nx, ny, gx, gy))
    border = border_copies(nx, ny, gx, gy, faces, halo, corners, send, recv)
    trade = trade_copies(nx, gx, gy, cotangent, returned, tsend, trecv)
    start_border(border)
    for copy in trade:
        copy.start()
    keep_own(nx, gx, cotangent, returned)
    wait_border(border)
    for copy in trade:
        copy.wait()


def late_kernel(
    nx, ny, faces, sending, sums, halo, corners, coarse, total,
    pair_in, line_in, row_in, pair_out, pair_sum, pair_send, line_sum, line_send, send, recv, tsend, trecv, ssend, srecv,
):
    gx, gy = lax.axis_index("gx"), lax.axis_index("gy")
    core, line, lines = lax.rem(gy, 2), gy // 2, ny // 2
    half = sums.shape[0] // 2
    part = half // lines
    unit = part // nx
    mate = (gx, gy + 1 - 2 * core)
    beside = [lax.rem(line + k, lines) for k in range(1, lines)]
    along = [lax.rem(gx + k, nx) for k in range(1, nx)]
    greet(around(nx, ny, gx, gy) + [mate] + [(gx, 2 * b + core) for b in beside])

    def copy_to(at, source, place, device):
        return pltpu.make_async_remote_copy(
            src_ref=source, dst_ref=place, send_sem=ssend.at[at], recv_sem=srecv.at[at],
            device_id=device, device_id_type=MESH,
        )

    def run(copies):
        for copy in copies:
            copy.start()
        for copy in copies:
            copy.wait()

    border = border_copies(nx, ny, gx, gy, faces, halo, corners, send, recv)
    trade = trade_copies(nx, gx, gy, sending, coarse, tsend, trecv)
    pair_out[...] = sums[at_rows((1 - core) * half, half)].astype(BF)
    first = copy_to(0, pair_out, pair_in, mate)
    first.start()
    start_border(border)
    for copy in trade:
        copy.start()
    keep_own(nx, gx, sending, coarse)
    first.wait()
    pair_sum[...] = sums[at_rows(core * half, half)] + pair_in[...].astype(F32)
    pair_send[...] = pair_sum[...].astype(BF)
    run([
        copy_to(1 + k, pair_send.at[at_rows(b * part, part)], line_in.at[k], (gx, 2 * b + core))
        for k, b in enumerate(beside)
    ])
    added = pair_sum[at_rows(line * part, part)]
    for k in range(lines - 1):
        added = added + line_in[k].astype(F32)
    line_sum[...] = added
    line_send[...] = added.astype(BF)
    base = lines
    run([
        copy_to(base + k, line_send.at[at_rows(a * unit, unit)], row_in.at[k], (a, gy))
        for k, a in enumerate(along)
    ])
    added = line_sum[at_rows(gx * unit, unit)]
    for k in range(nx - 1):
        added = added + row_in[k].astype(F32)
    start = core * half + line * part
    mine = at_rows(start + gx * unit, unit)
    total[mine] = added.astype(BF)
    base = base + nx - 1
    spread = [copy_to(base + k, total.at[mine], total.at[mine], (a, gy)) for k, a in enumerate(along)]
    for copy in spread:
        copy.start()
    base = base + nx - 1
    across = []
    for step in range(nx):
        if step:
            spread[step - 1].wait_recv()
        rows = at_rows(start + lax.rem(gx - step + nx, nx) * unit, unit)
        for b in beside:
            at = base + len(across)
            across.append(copy_to(at, total.at[rows], total.at[rows], (gx, 2 * b + core)))
            across[-1].start()
    base = base + nx * (lines - 1)
    last = []
    for k in range(lines):
        if k:
            for step in range(nx):
                across[step * (lines - 1) + k - 1].wait_recv()
        rows = at_rows(core * half + lax.rem(line - k + lines, lines) * part, part)
        last.append(copy_to(base + k, total.at[rows], total.at[rows], mate))
        last[-1].start()
    for copy in spread + across:
        copy.wait_send()
    for copy in last:
        copy.wait()
    wait_border(border)
    for copy in trade:
        copy.wait()


def swap_early(nx, ny, faces, cotangent):
    sems = [pltpu.SemaphoreType.DMA((8,))] * 2 + [pltpu.SemaphoreType.DMA((nx - 1,))] * 2
    return pl.pallas_call(
        functools.partial(early_kernel, nx, ny),
        out_shape=(
            jax.ShapeDtypeStruct((4, FACE, CH), BF),
            jax.ShapeDtypeStruct((4, SPAN, CH), BF),
            jax.ShapeDtypeStruct(cotangent.shape, BF),
        ),
        in_specs=[VM, VM],
        out_specs=(VM,) * 3,
        scratch_shapes=sems,
        compiler_params=pltpu.CompilerParams(
            collective_id=0, has_side_effects=True, vmem_limit_bytes=LIMIT
        ),
    )(faces, cotangent)


def swap_late(nx, ny, faces, sending, sums):
    rows = sums.shape[0]
    lines = ny // 2
    count = 2 * (lines + nx - 1) + nx * (lines - 1)
    sems = [pltpu.SemaphoreType.DMA((8,))] * 2 + [pltpu.SemaphoreType.DMA((nx - 1,))] * 2
    return pl.pallas_call(
        functools.partial(late_kernel, nx, ny),
        out_shape=(
            jax.ShapeDtypeStruct((4, FACE, CH), BF),
            jax.ShapeDtypeStruct((4, SPAN, CH), BF),
            jax.ShapeDtypeStruct(sending.shape, BF),
            jax.ShapeDtypeStruct(sums.shape, BF),
        ),
        in_specs=[VM] * 3,
        out_specs=(VM,) * 4,
        scratch_shapes=[
            pltpu.VMEM((rows // 2, CH), BF),
            pltpu.VMEM((lines - 1, rows // ny, CH), BF),
            pltpu.VMEM((nx - 1, rows // (nx * ny), CH), BF),
            pltpu.VMEM((rows // 2, CH), BF),
            pltpu.VMEM((rows // 2, CH), F32),
            pltpu.VMEM((rows // 2, CH), BF),
            pltpu.VMEM((rows // ny, CH), F32),
            pltpu.VMEM((rows // ny, CH), BF),
        ] + sems + [pltpu.SemaphoreType.DMA((count,))] * 2,
        compiler_params=pltpu.CompilerParams(
            collective_id=1, has_side_effects=True, vmem_limit_bytes=LIMIT
        ),
    )(faces, sending, sums)


def per_device(
    feats, voxel_mask, brick_coord, brick_count, route, conv_weight, down_weight, coarse_grad
):
    tiles_x = lax.axis_size("gx")
    tiles_y = lax.axis_size("gy")
    quarter = VOX // 8
    received = CAP * tiles_x
    params = pltpu.CompilerParams(vmem_limit_bytes=LIMIT)
    coord = brick_coord[0, 0]
    target = route[0, 0, :, 0] * CAP + route[0, 0, :, 1]
    feats = feats[0, 0]

    faces, mask = pl.pallas_call(
        face_kernel,
        out_shape=(
            jax.ShapeDtypeStruct((4, FACE, CH), BF),
            jax.ShapeDtypeStruct((SLOTS, VOX, CH), BF),
        ),
        in_specs=[SM, SM, VM, VM],
        out_specs=(VM, VM),
        scratch_shapes=[FACES, pltpu.VMEM((VOX, SLOTS), BF)],
        compiler_params=params,
    )(coord, brick_count[0, 0], feats, voxel_mask[0, 0])
    halo, corners, returned = swap_early(
        tiles_x, tiles_y, faces, coarse_grad.reshape(received * quarter, CH)
    )
    returned = returned.reshape(received, quarter, CH)
    each = -(-35 * CH // (tiles_x * tiles_y))
    padded = -(-each // 16) * 16 * tiles_x * tiles_y
    sending, grad_pre, grad_faces, sums = pl.pallas_call(
        main_kernel,
        out_shape=(
            jax.ShapeDtypeStruct((received, quarter, CH), BF),
            jax.ShapeDtypeStruct((SLOTS, VOX, CH), BF),
            jax.ShapeDtypeStruct((4, FACE, CH), BF),
            jax.ShapeDtypeStruct((padded, CH), F32),
        ),
        in_specs=[SM, SM] + [VM] * 7,
        out_specs=(VM,) * 4,
        scratch_shapes=[
            VOLUME, *PAIR, FACES,
            pltpu.VMEM((CH, 27 * CH), F32),
            pltpu.VMEM((SLOTS * quarter, CH), BF),
            pltpu.VMEM((SLOTS * quarter, 8 * CH), F32),
            pltpu.VMEM((SLOTS * quarter, 8 * CH), BF),
            pltpu.VMEM((VOX, CH), F32),
            pltpu.VMEM((VOX, CH), F32),
        ],
        compiler_params=params,
        cost_estimate=pl.CostEstimate(
            flops=4 * SLOTS * VOX * 27 * CH * CH, bytes_accessed=16 << 20, transcendentals=0
        ),
    )(
        coord, target, feats, mask, halo, corners, returned, conv_weight, down_weight,
    )
    grad_halo, grad_corners, coarse, total = swap_late(
        tiles_x, tiles_y, grad_faces, sending.reshape(received * quarter, CH), sums
    )
    coarse = coarse.reshape(1, 1, received, quarter, CH)
    feat_grad = pl.pallas_call(
        back_kernel,
        out_shape=jax.ShapeDtypeStruct((SLOTS, VOX, CH), BF),
        in_specs=[SM] + [VM] * 5,
        out_specs=VM,
        scratch_shapes=[VOLUME, *PAIR, pltpu.VMEM((27 * CH, CH), BF)],
        compiler_params=params,
        cost_estimate=pl.CostEstimate(
            flops=2 * SLOTS * VOX * 27 * CH * CH, bytes_accessed=8 << 20, transcendentals=0
        ),
    )(coord, grad_pre, mask, grad_halo, grad_corners, conv_weight)
    total_slots = tiles_x * tiles_y * SLOTS
    conv_grad = total[: 27 * CH].astype(F32) * (1.0 / math.sqrt(total_slots * VOX))
    down_grad = total[27 * CH : 35 * CH].astype(F32) * (1.0 / math.sqrt(total_slots * VOX // 8))
    return (coarse, feat_grad[None, None], conv_grad, down_grad)


def solution(mesh):
    in_specs = (
        P("gx", "gy", None, None, None),
        P("gx", "gy", None, None),
        P("gx", "gy", None, None),
        P("gx", "gy", None),
        P("gx", "gy", None, None),
        P(),
        P(),
        P("gx", "gy", None, None, None),
    )
    out_specs = (P("gx", "gy", None, None, None), P("gx", "gy", None, None, None), P(), P())
    return jax.shard_map(
        per_device, mesh=mesh, in_specs=in_specs, out_specs=out_specs, check_vma=False
    )
```
